32 devices in a mesh: dp: 4 (over x, core), tensor: 8 (over z, y).
Axes of the slice: x: 2, y: 2, z: 4, core: 2. Of those that a mesh axis runs over, the one named last changes fastest.
Arguments:
- queries: bfloat16 [4, 4, 64, 8192], P('dp', None, None, 'tensor'), may hold values from -64 to 64
- slot_keys_values: bfloat16 [4, 4, 2, 64, 1024], P('dp'), may hold values from -8 to 8
- segment_ids: int32 [4, 4, 64], P('dp'), may hold values from 0 to 3, never falling along the last dimension, each value on 1 to 32 neighbouring positions
- residual_in: bfloat16 [4, 4, 64, 4224], P('dp', None, None, 'tensor'), may hold values from -6 to 6
- cotangent: bfloat16 [4, 4, 64, 4224], P('dp', None, None, 'tensor'), may hold values from -32 to 32
- out_weight: bfloat16 [8192, 4224], P('tensor', 'dp'), may hold values from -0.0625 to 0.0625
- live_mask: int32 [4], replicated, may hold values 0 or 1
- micro_counts: int32 [4], replicated, may hold values from 1 to 4
Outputs:
- block_residual: bfloat16 [4, 4, 64, 4224], P('dp', None, None, 'tensor')
- query_gradient: bfloat16 [4, 4, 64, 8192], P('dp', None, None, 'tensor')
- key_value_grad: bfloat16 [4, 4, 2, 64, 1024], P('dp')
- projection_weight_gradient: float32 [8192, 4224], P('tensor', 'dp')
The draws below stay inside these ranges and needn't reach their ends.
All inputs are finite; a program needn't handle non-finite values.
Results may differ from the reference program's by a relative error of at most 0.014.
Values may be sent and summed in bfloat16 or wider, within the bound.
No kernel may reach another device: no remote copies, remote signals or barrier semaphores. Data moves between devices by JAX's collectives and lax.ppermute only.
A program may use at most 128 MiB of HBM per device.

```python
import math
import jax
import jax.numpy as jnp
import numpy as np
from jax import lax

HEAD_SIZE = 128
QUERY_HEADS = 64
KEY_VALUE_HEADS = 8
DW = 4224
SLOT_TOKENS = 64
MICRO_SLOTS = 4
DATA_REPLICAS = 4
N_DP = 4
N_TENSOR = 8


def draw_together(key):
    query_key = jax.random.fold_in(key, 11)
    keyval_key = jax.random.fold_in(key, 12)
    shape_q = (DATA_REPLICAS, MICRO_SLOTS, SLOT_TOKENS, QUERY_HEADS * HEAD_SIZE)
    key_value_shape = (DATA_REPLICAS, MICRO_SLOTS, 2, SLOT_TOKENS, KEY_VALUE_HEADS * HEAD_SIZE)
    query_vals = jax.random.normal(query_key, shape_q, jnp.float32)
    keyval_vals = jax.random.normal(keyval_key, key_value_shape, jnp.float32)
    query_vals = jnp.clip(query_vals, -64.0, 64.0)
    keyval_vals = jnp.clip(keyval_vals, -8.0, 8.0)
    return (query_vals.astype(jnp.bfloat16), keyval_vals.astype(jnp.bfloat16))


def draw_queries(key, part):
    return draw_together(key)[0]


def draw_slot_keys_values(key, part):
    return draw_together(key)[1]


def set_ends(values, own_key, smallest, top_value):
    index_at = [jax.random.randint(jax.random.fold_in(own_key, axis), (), 0, length) for axis, length in enumerate(values.shape)]
    main_axis = values.shape.index(max(values.shape))
    beside = index_at[:main_axis] + [(index_at[main_axis] + 1) % values.shape[main_axis]] + index_at[main_axis + 1:]
    return values.at[tuple(index_at)].set(smallest).at[tuple(beside)].set(top_value)


def spiked(result, stream_key, source, target, blocks, factor):
    def block_of(dim):
        return (jnp.arange(result.shape[dim]) // (result.shape[dim] // blocks)).reshape((-1,) + (1,) * (result.ndim - 1 - dim))

    first = jax.random.permutation(stream_key, blocks)[block_of(target)]
    second = (block_of(target) + blocks // 2) % blocks
    return jnp.where((block_of(source) == first) | (block_of(source) == second), factor * result, result)


def block_levels(key, shape, shards, smallest, top_value):
    def one(position, shards_of):
        draws = jax.random.uniform(jax.random.fold_in(jax.random.fold_in(key, 6), position), (shards_of,), jnp.float32, smallest / len(shards), top_value / len(shards))
        return jnp.repeat(jnp.exp(draws), shape[position] // shards_of).reshape((-1,) + (1,) * (len(shape) - position - 1))

    factor_of = one(*shards[0])
    for cut in shards[1:]:
        factor_of = factor_of * one(*cut)
    return factor_of


def split_up(number_of, total, reach, skew):
    weights = [(1 << 20) // math.isqrt(grade ** skew) + 1 for grade in range(2, number_of + 1)]
    spare, given = total - reach - (number_of - 1), [1] * (number_of - 1)
    while spare > 0:
        candidates = [i for i in range(number_of - 1) if given[i] < reach]
        mass, remaining = sum([weights[i] for i in candidates]), spare
        for i in candidates:
            extra = min(reach - given[i], max(1, remaining * weights[i] // mass), spare)
            given[i] = given[i] + extra
            spare = spare - extra
    return np.array([reach] + given)


def ragged_sizes(rng, amount, total, reach, skew):
    if amount == 2:
        one = jax.random.randint(rng, (), max(1, total - reach), min(reach, total - 1) + 1)
        return jnp.stack([one, total - one])
    tallies = jnp.asarray(split_up(amount, total, reach, skew), jnp.int32)
    twos = (amount - 1) // 2
    source_of, receiver = tallies[1:1 + 2 * twos:2], tallies[2:2 + 2 * twos:2]
    slack = jnp.minimum(source_of - 1, reach - receiver)
    shifted = jax.random.randint(jax.random.fold_in(rng, 1), (twos,), 0, 1 << 20) % (slack + 1)
    tallies = tallies.at[1:1 + 2 * twos:2].set(source_of - shifted).at[2:2 + 2 * twos:2].set(receiver + shifted)
    return tallies[jax.random.permutation(jax.random.fold_in(rng, 2), amount)]


def gaussian(stream_key, shape, scale, reach, pieces=(), kind=jnp.bfloat16):
    level = block_levels(stream_key, shape, pieces, -0.22, 0.18) if pieces else 1.0
    drawn = jax.random.normal(stream_key, shape, jnp.float32) * scale * level
    return jnp.minimum(jnp.maximum(drawn, -reach), reach).astype(kind)


def bell_draw_with(stream_key, extent, spread, reach, pieces, heavy, dtype=jnp.bfloat16):
    result = spread * jax.random.normal(stream_key, extent, jnp.float32)
    if pieces:
        result = result * block_levels(stream_key, extent, pieces, -0.22, 0.18)
    return jnp.clip(spiked(result, jax.random.fold_in(stream_key, 3), *heavy), -reach, reach).astype(dtype)


def setup_inputs(seed: int = 0) -> dict:
    key_of = jax.random.split(jax.random.key(seed), 9)
    return {
        "queries": draw_queries(jax.random.fold_in(key_of[8], 71), 0),
        "slot_keys_values": draw_slot_keys_values(jax.random.fold_in(key_of[8], 71), 0),
        "segment_ids": jax.vmap(lambda own: jnp.searchsorted(jnp.cumsum(ragged_sizes(own, 4, SLOT_TOKENS, SLOT_TOKENS // 2, 1)), jnp.arange(SLOT_TOKENS), side="right"))(jax.random.split(key_of[2], DATA_REPLICAS * MICRO_SLOTS)).reshape((DATA_REPLICAS, MICRO_SLOTS, SLOT_TOKENS)).astype(jnp.int32),
        "residual_in": gaussian(key_of[3], (DATA_REPLICAS, MICRO_SLOTS, SLOT_TOKENS, DW), 1.0, 6.0, ((0, 4), (3, 8))),
        "cotangent": bell_draw_with(key_of[4], (DATA_REPLICAS, MICRO_SLOTS, SLOT_TOKENS, DW), N_DP, 32.0, ((0, 4), (3, 8)), (0, 3, 4, 2.0)),
        "out_weight": gaussian(key_of[5], (QUERY_HEADS * HEAD_SIZE, DW), (QUERY_HEADS * HEAD_SIZE) ** -0.5, 0.0625, ((0, 8), (1, 4))),
        "live_mask": set_ends((jax.random.randint(key_of[6], (DATA_REPLICAS,), 0, 5) < 4).astype(jnp.int32), jax.random.fold_in(key_of[6], 1), 0, 1),
        "micro_counts": set_ends(jax.random.randint(key_of[7], (DATA_REPLICAS,), 1, MICRO_SLOTS + 1), jax.random.fold_in(key_of[7], 1), 1, MICRO_SLOTS).astype(jnp.int32),
    }


def attend_slot(query, key_value_pair, segment):
    heads_per_group = QUERY_HEADS // KEY_VALUE_HEADS
    query_f = query.astype(jnp.float32).reshape(SLOT_TOKENS, QUERY_HEADS, HEAD_SIZE).transpose(1, 0, 2)
    key_value_float = key_value_pair.astype(jnp.float32).reshape(2, SLOT_TOKENS, KEY_VALUE_HEADS, HEAD_SIZE).transpose(0, 2, 1, 3)
    key_f = jnp.repeat(key_value_float[0], heads_per_group, axis=0)
    value_f = jnp.repeat(key_value_float[1], heads_per_group, axis=0)
    positions = jnp.arange(SLOT_TOKENS)
    allowed = (positions[None, :] <= positions[:, None]) & (segment[:, None] == segment[None, :])
    scores = jnp.einsum('hqd,hkd->hqk', query_f, key_f, precision=lax.Precision.HIGHEST) / math.sqrt(HEAD_SIZE)
    masked = jnp.where(allowed[None], scores, -jnp.inf)
    top_score = lax.optimization_barrier(jnp.max(masked, axis=-1, keepdims=True))
    expo = jnp.where(allowed[None], jnp.exp(masked - top_score), 0.0)
    probs = expo / lax.optimization_barrier(jnp.sum(expo, axis=-1, keepdims=True))
    rounded = lax.optimization_barrier(probs.astype(jnp.bfloat16)).astype(jnp.float32)
    context = jnp.einsum('hqk,hkd->qhd', rounded, value_f, precision=lax.Precision.HIGHEST)
    context = context.astype(jnp.bfloat16).reshape(SLOT_TOKENS, QUERY_HEADS * HEAD_SIZE)
    return (context, probs, rounded, query_f, key_f, value_f)

def backward_slot(query, key_value_pair, segment, context_grad):
    context, probs, rounded, query_f, key_f, value_f = attend_slot(query, key_value_pair, segment)
    grad_heads = context_grad.reshape(SLOT_TOKENS, QUERY_HEADS, HEAD_SIZE).transpose(1, 0, 2)
    prob_grad = jnp.einsum('hqd,hkd->hqk', grad_heads, value_f, precision=lax.Precision.HIGHEST)
    delta = lax.optimization_barrier(jnp.sum(prob_grad * probs, axis=-1, keepdims=True))
    score_grad = probs * (prob_grad - delta)
    query_gradient = jnp.einsum('hqk,hkd->qhd', score_grad, key_f, precision=lax.Precision.HIGHEST) / math.sqrt(HEAD_SIZE)
    key_term = jnp.einsum('hqk,hqd->hkd', score_grad, query_f, precision=lax.Precision.HIGHEST) / math.sqrt(HEAD_SIZE)
    value_term = jnp.einsum('hqk,hqd->hkd', rounded, grad_heads, precision=lax.Precision.HIGHEST)
    addend_terms = jnp.stack([key_term, value_term], axis=0)
    addend_terms = lax.optimization_barrier(addend_terms.astype(jnp.bfloat16)).astype(jnp.float32)
    reduced_total = addend_terms.reshape(2, KEY_VALUE_HEADS, QUERY_HEADS // KEY_VALUE_HEADS, SLOT_TOKENS, HEAD_SIZE).sum(axis=2)
    key_value_gradient = reduced_total.transpose(0, 2, 1, 3).reshape(2, SLOT_TOKENS, KEY_VALUE_HEADS * HEAD_SIZE).astype(jnp.bfloat16)
    return (query_gradient.reshape(SLOT_TOKENS, QUERY_HEADS * HEAD_SIZE).astype(jnp.bfloat16), key_value_gradient)

def reference(queries, slot_keys_values, segment_ids, residual_in, cotangent, out_weight, live_mask, micro_counts):
    slot_entries = DATA_REPLICAS * MICRO_SLOTS
    query_flat = queries.reshape(slot_entries, SLOT_TOKENS, QUERY_HEADS * HEAD_SIZE)
    key_value_flattened = slot_keys_values.reshape(slot_entries, 2, SLOT_TOKENS, KEY_VALUE_HEADS * HEAD_SIZE)
    segment_flat = segment_ids.reshape(slot_entries, SLOT_TOKENS)
    context = lax.map(lambda ops: attend_slot(ops[0], ops[1], ops[2])[0], (query_flat, key_value_flattened, segment_flat))
    heads_here = QUERY_HEADS // N_TENSOR
    context_rows = context.reshape(slot_entries * SLOT_TOKENS, N_TENSOR, heads_here * HEAD_SIZE).transpose(1, 0, 2)
    weight_groups = out_weight.reshape(N_TENSOR, heads_here * HEAD_SIZE, DW)

    def add_group(running, group_idx):
        term = jnp.dot(context_rows[group_idx], weight_groups[group_idx], preferred_element_type=jnp.float32)
        term = lax.optimization_barrier(term.astype(jnp.bfloat16)).astype(jnp.float32)
        return (running + term, None)
    reduced_total, _ = lax.scan(add_group, jnp.zeros((slot_entries * SLOT_TOKENS, DW), jnp.float32), jnp.arange(N_TENSOR))
    block_residual = (residual_in.astype(jnp.float32) + reduced_total.reshape(DATA_REPLICAS, MICRO_SLOTS, SLOT_TOKENS, DW)).astype(jnp.bfloat16)
    live_total = jnp.maximum(jnp.sum(live_mask * micro_counts), 1)
    slot_live = (jnp.arange(MICRO_SLOTS)[None, :] < micro_counts[:, None]) & (live_mask[:, None] > 0)
    slot_weight = slot_live.astype(jnp.float32) / live_total.astype(jnp.float32)
    scaled_cot = (cotangent.astype(jnp.float32) * slot_weight[:, :, None, None]).astype(jnp.bfloat16)
    cot_rows = scaled_cot.reshape(slot_entries * SLOT_TOKENS, DW)
    context_grad = jnp.dot(cot_rows, out_weight.T, preferred_element_type=jnp.float32)
    projection_weight_gradient = jnp.dot(context.reshape(slot_entries * SLOT_TOKENS, QUERY_HEADS * HEAD_SIZE).T, cot_rows, preferred_element_type=jnp.float32)
    query_gradient, key_value_gradient = lax.map(lambda ops: backward_slot(ops[0], ops[1], ops[2], ops[3]), (query_flat, key_value_flattened, segment_flat, context_grad.reshape(slot_entries, SLOT_TOKENS, QUERY_HEADS * HEAD_SIZE)))
    return (block_residual, query_gradient.reshape(DATA_REPLICAS, MICRO_SLOTS, SLOT_TOKENS, QUERY_HEADS * HEAD_SIZE), key_value_gradient.reshape(DATA_REPLICAS, MICRO_SLOTS, 2, SLOT_TOKENS, KEY_VALUE_HEADS * HEAD_SIZE), projection_weight_gradient)
```

```python
import functools
import math

import jax
import jax.numpy as jnp
from jax import lax
from jax.experimental import pallas as pl
from jax.experimental.pallas import tpu as pltpu
from jax.sharding import PartitionSpec as P

HEAD_SIZE = 128
QUERY_HEADS = 64
KEY_VALUE_HEADS = 8
BF = jnp.bfloat16
F32 = jnp.float32
VMEM = pl.BlockSpec(memory_space=pltpu.VMEM)
SMEM = pl.BlockSpec(memory_space=pltpu.SMEM)
NT = (((1,), (1,)), ((), ()))
TN = (((0,), (0,)), ((), ()))
NN = (((1,), (0,)), ((), ()))
LIMIT = 48 * 1024 * 1024


def dot(a, b, dims=NN):
    return lax.dot_general(a, b, dims, preferred_element_type=F32)


def call(kernel, out_shape, in_specs, flops, moved, scratch=(), **grid):
    return pl.pallas_call(
        kernel,
        out_shape=out_shape,
        in_specs=in_specs,
        scratch_shapes=scratch,
        cost_estimate=pl.CostEstimate(flops=flops, bytes_accessed=moved, transcendentals=0),
        compiler_params=pltpu.CompilerParams(vmem_limit_bytes=LIMIT),
        **grid,
    )


def stack_heads(rows, heads):
    return jnp.concatenate(
        [rows[:, h * HEAD_SIZE : (h + 1) * HEAD_SIZE] for h in range(heads)], axis=0
    )


def forward_kernel(heads, q_ref, key_value_ref, seg_ref, context_ref, probs_ref):
    slots, length = q_ref.shape[:2]
    row = lax.broadcasted_iota(jnp.int32, (length, length), 0)
    col = lax.broadcasted_iota(jnp.int32, (length, length), 1)
    for m in range(slots):
        seg = jnp.broadcast_to(seg_ref[m : m + 1, :].astype(F32), (length, length))
        allowed = (col <= row) & (seg == seg.T)
        q = stack_heads(q_ref[m], heads)
        scores = dot(q, key_value_ref[m, 0], NT) * (1.0 / math.sqrt(HEAD_SIZE))
        scores = scores.reshape(heads, length, length)
        masked = jnp.where(allowed[None], scores, -jnp.inf)
        expo = jnp.exp(masked - jnp.max(masked, axis=-1, keepdims=True))
        probs = expo / jnp.sum(expo, axis=-1, keepdims=True)
        probs = probs.reshape(heads * length, length)
        probs_ref[m] = probs
        context = dot(probs.astype(BF), key_value_ref[m, 1]).astype(BF)
        for h in range(heads):
            context_ref[m * length : (m + 1) * length, h * HEAD_SIZE : (h + 1) * HEAD_SIZE] = (
                context[h * length : (h + 1) * length]
            )


def backward_kernel(
    heads, own_ref, got_ref, q_ref, key_value_ref, probs_ref, query_grad_ref, key_value_grad_ref
):
    slots, length = q_ref.shape[:2]
    scale = 1.0 / math.sqrt(HEAD_SIZE)
    for m in range(slots):
        rows = slice(m * length, (m + 1) * length)
        grad = (own_ref[rows, :] + got_ref[rows, :].astype(F32)).astype(BF)
        grad = stack_heads(grad, heads)
        q = stack_heads(q_ref[m], heads)
        key, value = key_value_ref[m, 0], key_value_ref[m, 1]
        probs = probs_ref[m]
        prob_grad = dot(grad, value, NT)
        delta = jnp.sum(prob_grad * probs, axis=-1, keepdims=True)
        score_grad = probs * (prob_grad - delta)
        high = score_grad.astype(BF)
        low = (score_grad - high.astype(F32)).astype(BF)
        query_grad = ((dot(high, key) + dot(low, key)) * scale).astype(BF)
        for h in range(heads):
            query_grad_ref[m, :, h * HEAD_SIZE : (h + 1) * HEAD_SIZE] = query_grad[
                h * length : (h + 1) * length
            ]
        key_grad = (dot(high, q, TN) + dot(low, q, TN)) * scale
        key_value_grad_ref[m, 0] = key_grad.astype(BF)
        key_value_grad_ref[m, 1] = dot(probs.astype(BF), grad, TN).astype(BF)


def project_kernel(parts, split, half_ref, block_ref, own_ref, other_ref, weight_ref, *refs):
    outs, context = refs[:-1], refs[-1]
    tokens = own_ref.shape[0]
    features = outs[0].shape[0] + outs[1].shape[0]
    context[:tokens, :] = own_ref[...]
    context[tokens:, :] = other_ref[...]
    for k in range(parts):
        at = pl.multiple_of(block_ref[k] * features, 16)
        rows = pl.multiple_of(half_ref[k] * tokens, 16)
        block = dot(weight_ref[pl.ds(at, features), :], context[pl.ds(rows, tokens), :], NT)
        block = block.astype(BF)
        outs[2 * k][...] = block[:split]
        outs[2 * k + 1][...] = block[split:]


def context_grad_kernel(half_ref, block_ref, *refs):
    shards, (weight_ref, own_ref, other_ref, total) = refs[:-4], refs[-4:]
    total[...] = jnp.zeros_like(total)
    tokens = own_ref.shape[0]
    for k in range(len(shards) // 2):
        base = block_ref[k] * (shards[0].shape[0] + shards[1].shape[0])
        rows = pl.ds(pl.multiple_of(half_ref[k] * tokens, 16), tokens)
        term = None
        for shard in shards[2 * k : 2 * k + 2]:
            at = pl.multiple_of(base, 16)
            part = dot(shard[...], weight_ref[pl.ds(at, shard.shape[0]), :], TN)
            term = part if term is None else term + part
            base = base + shard.shape[0]
        total[rows, :] += term
    own_ref[...] = total[:tokens, :]
    other_ref[...] = total[tokens:, :].astype(BF)


def weight_grad_kernel(half_ref, block_ref, *refs):
    shards = refs[:-6]
    context_own, context_other, own_ref, other_ref, total, context = refs[-6:]
    tokens = context_own.shape[0]
    context[:tokens, :] = context_own[...]
    context[tokens:, :] = context_other[...]
    total[...] = jnp.zeros_like(total)
    for k in range(len(shards) // 2):
        base = block_ref[k] * (shards[0].shape[0] + shards[1].shape[0])
        rows = pl.ds(pl.multiple_of(half_ref[k] * tokens, 16), tokens)
        for shard in shards[2 * k : 2 * k + 2]:
            at = pl.ds(pl.multiple_of(base, 16), shard.shape[0])
            total[at, :] += dot(shard[...], context[rows, :])
            base = base + shard.shape[0]
    own = own_ref.shape[0]
    own_ref[...] = total[:own, :]
    other_ref[...] = total[own:, :].astype(BF)


def place_kernel(col_ref, *refs):
    shards, out_ref = refs[:-1], refs[-1]
    for k, shard in enumerate(shards):
        at = pl.multiple_of(col_ref[k] * HEAD_SIZE, HEAD_SIZE)
        out_ref[:, pl.ds(at, HEAD_SIZE)] = shard[...]


class Ring:
    def __init__(self, axis, size):
        self.axis, self.size = axis, size
        self.order = list(range(0, size, 2)) + list(range(1, size, 2))[::-1]
        self.up = [(self.order[i], self.order[(i + 1) % size]) for i in range(size)]
        self.down = [(b, a) for a, b in self.up]
        place = [self.order.index(t) for t in range(size)]
        table = [[self.order[(place[t] + k) % size] for k in range(size)] for t in range(size)]
        self.table = jnp.array(table, jnp.int32)

    def ids(self):
        return self.table[lax.axis_index(self.axis)]

    def send(self, arrays, way):
        return [lax.ppermute(a, self.axis, way) for a in arrays]

    def gather(self, pair):
        n = self.size
        out = [None] * n
        out[0] = a = b = list(pair)
        for step in range(1, n // 2):
            a, b = self.send(a, self.up), self.send(b, self.down)
            out[n - step], out[step] = a, b
        out[n // 2] = self.send(a[:1], self.up) + self.send(b[1:], self.down)
        return out

    def scatter_sum(self, pairs):
        n = self.size
        far = pairs[n // 2]
        a = [far[0], None]
        b = [None, far[1]]
        for step in range(n // 2 - 1, -1, -1):
            a = [None if v is None else lax.ppermute(v, self.axis, self.up) for v in a]
            b = [None if v is None else lax.ppermute(v, self.axis, self.down) for v in b]
            if step:
                add = lambda mine, got: mine if got is None else mine + got
                a = [add(m, g) for m, g in zip(pairs[step], a)]
                b = [add(m, g) for m, g in zip(pairs[n - step], b)]
        return [
            p.astype(F32) + u.astype(F32) + d.astype(F32) for p, u, d in zip(pairs[0], a, b)
        ]


def slot_weights(live_mask, micro_counts, slots):
    replica = lax.axis_index("dp")
    pick = jnp.arange(live_mask.shape[0]) == replica
    my_live = jnp.sum(jnp.where(pick, live_mask, 0))
    my_count = jnp.sum(jnp.where(pick, micro_counts, 0))
    live_total = jnp.maximum(jnp.sum(live_mask * micro_counts), 1)
    slot_live = (jnp.arange(slots) < my_count) & (my_live > 0)
    return slot_live.astype(F32) / live_total.astype(F32)


def by_activations(
    dp_size,
    tensor_size,
    queries,
    slot_keys_values,
    segment_ids,
    residual_in,
    cotangent,
    out_weight,
    live_mask,
    micro_counts,
):
    pairs = dp_size // 2
    inner = tensor_size // pairs
    _, slots, length, width = queries.shape
    features = residual_in.shape[3]
    heads = width // HEAD_SIZE
    tokens = slots * length
    dp_idx, tensor_idx = lax.axis_index("dp"), lax.axis_index("tensor")
    pair_idx, core = dp_idx // 2, dp_idx % 2
    both = ("dp", "tensor")

    def device(x, c, t):
        return (2 * x + c) * tensor_size + t

    every = [(x, c, t) for x in range(pairs) for c in range(2) for t in range(tensor_size)]
    swap_cores = [(2 * x + c, 2 * x + 1 - c) for x in range(pairs) for c in range(2)]
    swap_pairs = [(2 * x + c, 2 * (1 - x) + c) for x in range(pairs) for c in range(2)]
    turn = [
        (device(x, c, t), device(t // inner, c, x * inner + t % inner)) for x, c, t in every
    ]
    ring = Ring("tensor", tensor_size)
    ids = ring.ids()
    half_ids = (ids // inner) ^ pair_idx
    in_block = ids % inner
    per_core = inner // 2
    block_ids = ((in_block // per_core) ^ core) * per_core + in_block % per_core
    split = (features // 2 + 15) // 16 * 16

    weight = slot_weights(live_mask, micro_counts, slots)
    scaled = (cotangent[0].astype(F32) * weight[:, None, None]).astype(BF)
    scaled = scaled.reshape(tokens, features).T
    scaled = lax.ppermute(scaled, both, turn)
    shards = ring.gather([scaled[:split], scaled[split:]])

    weight_own = out_weight.T
    weight_rows = jnp.concatenate([weight_own, lax.ppermute(weight_own, "dp", swap_cores)], axis=0)

    key_value = lax.dynamic_slice_in_dim(
        slot_keys_values[0], tensor_idx * HEAD_SIZE, HEAD_SIZE, axis=3
    )
    context, probs = call(
        functools.partial(forward_kernel, heads),
        (
            jax.ShapeDtypeStruct((tokens, width), BF),
            jax.ShapeDtypeStruct((slots, heads * length, length), F32),
        ),
        [VMEM] * 3,
        4 * tokens * width * length,
        4 * tokens * width * 2,
    )(queries[0], key_value, segment_ids[0])
    context_other = lax.ppermute(context, "dp", swap_pairs)

    piece = [
        jax.ShapeDtypeStruct((split, tokens), BF),
        jax.ShapeDtypeStruct((features - split, tokens), BF),
    ]
    big = 2 * 2 * tokens * width * inner * features
    partial = call(
        functools.partial(project_kernel, tensor_size, split),
        piece * tensor_size,
        [SMEM, SMEM, VMEM, VMEM, VMEM],
        big,
        2 * inner * features * width,
        [pltpu.VMEM((2 * tokens, width), BF)],
    )(half_ids, block_ids, context, context_other, weight_rows)
    summed = ring.scatter_sum([partial[2 * k : 2 * k + 2] for k in range(tensor_size)])
    summed = jnp.concatenate([s.astype(BF) for s in summed], axis=0)
    summed = lax.ppermute(summed, both, turn)
    block_residual = (
        residual_in[0].astype(F32) + summed.T.reshape(slots, length, features).astype(F32)
    ).astype(BF)[None]

    flat = [piece for pair in shards for piece in pair]
    grad_own, grad_other = call(
        context_grad_kernel,
        (jax.ShapeDtypeStruct((tokens, width), F32), jax.ShapeDtypeStruct((tokens, width), BF)),
        [SMEM, SMEM] + [VMEM] * (len(flat) + 1),
        big,
        2 * inner * features * width,
        [pltpu.VMEM((2 * tokens, width), F32)],
    )(half_ids, block_ids, *flat, weight_rows)
    grad_got = lax.ppermute(grad_other, "dp", swap_pairs)
    query_gradient, key_value_part = call(
        functools.partial(backward_kernel, heads),
        (
            jax.ShapeDtypeStruct((slots, length, width), BF),
            jax.ShapeDtypeStruct((slots, 2, length, HEAD_SIZE), BF),
        ),
        [VMEM] * 5,
        14 * tokens * width * length,
        8 * tokens * width * 2,
    )(grad_own, grad_got, queries[0], key_value, probs)

    own_rows = weight_own.shape[0]
    weight_grad, weight_grad_other = call(
        weight_grad_kernel,
        (
            jax.ShapeDtypeStruct((own_rows, width), F32),
            jax.ShapeDtypeStruct((own_rows, width), BF),
        ),
        [SMEM, SMEM] + [VMEM] * (len(flat) + 2),
        big,
        6 * own_rows * width,
        [pltpu.VMEM((2 * own_rows, width), F32), pltpu.VMEM((2 * tokens, width), BF)],
    )(half_ids, block_ids, *flat, context, context_other)
    weight_grad_got = lax.ppermute(weight_grad_other, "dp", swap_cores)
    weight_grad = (weight_grad + weight_grad_got.astype(F32)).T

    rows = slots * 2 * length
    part = key_value_part.reshape(rows, HEAD_SIZE)
    parts = ring.gather([part[: rows // 2], part[rows // 2 :]])
    top, bottom = [
        call(
            place_kernel,
            jax.ShapeDtypeStruct((rows // 2, KEY_VALUE_HEADS * HEAD_SIZE), BF),
            [SMEM] + [VMEM] * tensor_size,
            0,
            2 * rows * KEY_VALUE_HEADS * HEAD_SIZE,
        )(ids, *[pair[i] for pair in parts])
        for i in range(2)
    ]
    key_value_gradient = jnp.concatenate([top, bottom], axis=0).reshape(
        1, slots, 2, length, KEY_VALUE_HEADS * HEAD_SIZE
    )
    return block_residual, query_gradient[None], key_value_gradient, weight_grad


def attention_backward(query_f, key_f, value_f, probs, rounded, grad_heads):
    prob_grad = jnp.einsum("mhqd,mhkd->mhqk", grad_heads, value_f, precision=lax.Precision.HIGHEST)
    delta = jnp.sum(prob_grad * probs, axis=-1, keepdims=True)
    score_grad = probs * (prob_grad - delta)
    query_gradient = jnp.einsum(
        "mhqk,mhkd->mhqd", score_grad, key_f, precision=lax.Precision.HIGHEST
    ) / math.sqrt(HEAD_SIZE)
    key_term = jnp.einsum(
        "mhqk,mhqd->mhkd", score_grad, query_f, precision=lax.Precision.HIGHEST
    ) / math.sqrt(HEAD_SIZE)
    value_term = jnp.einsum("mhqk,mhqd->mhkd", rounded, grad_heads, precision=lax.Precision.HIGHEST)
    return (query_gradient, key_term, value_term)


def by_weights(
    queries,
    slot_keys_values,
    segment_ids,
    residual_in,
    cotangent,
    out_weight,
    live_mask,
    micro_counts,
):
    tensor_size = lax.axis_size("tensor")
    heads_here = QUERY_HEADS // tensor_size
    heads_per_group = QUERY_HEADS // KEY_VALUE_HEADS
    tensor_idx = lax.axis_index("tensor")
    replica_idx = lax.axis_index("dp")
    query_here = queries[0]
    slot_total_count = query_here.shape[0]
    sequence_length = query_here.shape[1]
    local_feats = residual_in.shape[3]
    key_value_local = slot_keys_values[0].reshape(
        slot_total_count, 2, sequence_length, KEY_VALUE_HEADS, HEAD_SIZE
    )
    segments = segment_ids[0]
    head_ids = tensor_idx * heads_here + jnp.arange(heads_here)
    key_value_head_rows = head_ids // heads_per_group
    query_heads = query_here.reshape(
        slot_total_count, sequence_length, heads_here, HEAD_SIZE
    ).transpose(0, 2, 1, 3)
    key_head_rows = jnp.take(key_value_local[:, 0], key_value_head_rows, axis=2).transpose(
        0, 2, 1, 3
    )
    value_heads = jnp.take(key_value_local[:, 1], key_value_head_rows, axis=2).transpose(0, 2, 1, 3)
    positions = jnp.arange(sequence_length)
    allowed = (positions[None, :] <= positions[:, None])[None] & (
        segments[:, :, None] == segments[:, None, :]
    )
    allowed = allowed[:, None]
    scores = jnp.einsum(
        "mhqd,mhkd->mhqk", query_heads, key_head_rows, preferred_element_type=jnp.float32
    ) / math.sqrt(HEAD_SIZE)
    masked = jnp.where(allowed, scores, -jnp.inf)
    top_score = jnp.max(masked, axis=-1, keepdims=True)
    expo = jnp.where(allowed, jnp.exp(masked - top_score), 0.0)
    probs = expo / jnp.sum(expo, axis=-1, keepdims=True)
    probs_low = probs.astype(jnp.bfloat16)
    context = jnp.einsum(
        "mhqk,mhkd->mqhd", probs_low, value_heads, preferred_element_type=jnp.float32
    )
    context = context.astype(jnp.bfloat16).reshape(
        slot_total_count, sequence_length, heads_here * HEAD_SIZE
    )
    context_rows = context.reshape(slot_total_count * sequence_length, heads_here * HEAD_SIZE)
    weight_rows = lax.all_gather(out_weight, "dp", axis=1, tiled=True)
    reduced_total = lax.psum_scatter(
        jnp.einsum(
            "hd,nh->dn", weight_rows, context_rows, preferred_element_type=jnp.float32
        ).astype(jnp.bfloat16),
        "tensor",
        scatter_dimension=0,
        tiled=True,
    ).astype(jnp.float32)
    reduced_total = reduced_total.transpose(1, 0).reshape(
        slot_total_count, sequence_length, local_feats
    )
    block_residual = (residual_in[0].astype(jnp.float32) + reduced_total).astype(jnp.bfloat16)[None]
    replica_pick = jnp.arange(live_mask.shape[0]) == replica_idx
    my_live = jnp.sum(jnp.where(replica_pick, live_mask, 0))
    my_count = jnp.sum(jnp.where(replica_pick, micro_counts, 0))
    live_total = jnp.maximum(jnp.sum(live_mask * micro_counts), 1)
    slot_live = (jnp.arange(slot_total_count) < my_count) & (my_live > 0)
    slot_weight = slot_live.astype(jnp.float32) / live_total.astype(jnp.float32)
    scaled_cot = (cotangent[0].astype(jnp.float32) * slot_weight[:, None, None]).astype(
        jnp.bfloat16
    )
    weight_back = lax.all_gather(out_weight, "dp", axis=1, tiled=True)
    shard_piece = lax.all_gather(scaled_cot, "tensor", axis=2, tiled=True)
    grad_piece = jnp.einsum("msh,msd->hd", context, shard_piece, preferred_element_type=jnp.float32)
    grad_rows = grad_piece
    context_grad = jnp.einsum(
        "msd,hd->msh", shard_piece, weight_back, preferred_element_type=jnp.float32
    )
    grad_rows, context_grad = (grad_rows, context_grad)
    projection_weight_gradient = lax.psum_scatter(
        grad_rows.astype(jnp.bfloat16), "dp", scatter_dimension=1, tiled=True
    ).astype(jnp.float32)
    grad_heads = context_grad.reshape(
        slot_total_count, sequence_length, heads_here, HEAD_SIZE
    ).transpose(0, 2, 1, 3)
    query_f = query_heads.astype(jnp.float32)
    key_f = key_head_rows.astype(jnp.float32)
    value_f = value_heads.astype(jnp.float32)
    rounded = probs_low.astype(jnp.float32)
    query_gradient, key_term, value_term = attention_backward(
        query_f, key_f, value_f, probs, rounded, grad_heads
    )
    query_out = (
        query_gradient.transpose(0, 2, 1, 3)
        .reshape(slot_total_count, sequence_length, heads_here * HEAD_SIZE)
        .astype(jnp.bfloat16)[None]
    )
    addend_terms = (
        jnp.stack([key_term, value_term], axis=1).astype(jnp.bfloat16).astype(jnp.float32)
    )
    head_choice = (key_value_head_rows[:, None] == jnp.arange(KEY_VALUE_HEADS)[None, :]).astype(
        jnp.float32
    )
    positioned = jnp.einsum(
        "mchsd,hk->mcskd", addend_terms, head_choice, precision=lax.Precision.HIGHEST
    )
    positioned = positioned.reshape(
        slot_total_count, 2, sequence_length, KEY_VALUE_HEADS * HEAD_SIZE
    )
    keyval_sum = lax.psum(positioned.astype(jnp.bfloat16), "tensor")
    key_value_gradient = keyval_sum[None]
    return (block_residual, query_out, key_value_gradient, projection_weight_gradient)


def solution(mesh):
    dp_size, tensor_size = mesh.shape["dp"], mesh.shape["tensor"]
    regular = dp_size == 4 and tensor_size % dp_size == 0
    regular = regular and tensor_size == KEY_VALUE_HEADS
    per_device = (
        functools.partial(by_activations, dp_size, tensor_size) if regular else by_weights
    )
    placed = (
        P("dp", None, None, "tensor"),
        P("dp", None, None, None, None),
        P("dp", None, None),
        P("dp", None, None, "tensor"),
        P("dp", None, None, "tensor"),
        P("tensor", "dp"),
        P(),
        P(),
    )
    return jax.shard_map(
        per_device,
        mesh=mesh,
        in_specs=placed,
        out_specs=(
            P("dp", None, None, "tensor"),
            P("dp", None, None, "tensor"),
            P("dp", None, None, None, None),
            P("tensor", "dp"),
        ),
        check_vma=False,
    )
```

```python
import functools
import math

import jax
import jax.numpy as jnp
from jax import lax
from jax.experimental import pallas as pl
from jax.experimental.pallas import tpu as pltpu
from jax.sharding import PartitionSpec as P

HEAD_SIZE = 128
QUERY_HEADS = 64
KEY_VALUE_HEADS = 8
BF = jnp.bfloat16
F32 = jnp.float32
VMEM = pl.BlockSpec(memory_space=pltpu.VMEM)
SMEM = pl.BlockSpec(memory_space=pltpu.SMEM)
NT = (((1,), (1,)), ((), ()))
TN = (((0,), (0,)), ((), ()))
NN = (((1,), (0,)), ((), ()))
LIMIT = 28 * 1024 * 1024


def dot(a, b, dims=NN):
    return lax.dot_general(a, b, dims, preferred_element_type=F32)


def call(kernel, out_shape, in_specs, flops, moved, scratch=(), **grid):
    return pl.pallas_call(
        kernel,
        out_shape=out_shape,
        in_specs=in_specs,
        scratch_shapes=scratch,
        cost_estimate=pl.CostEstimate(flops=flops, bytes_accessed=moved, transcendentals=0),
        compiler_params=pltpu.CompilerParams(vmem_limit_bytes=LIMIT),
        **grid,
    )


def stack_heads(rows, heads):
    return jnp.concatenate(
        [rows[:, h * HEAD_SIZE : (h + 1) * HEAD_SIZE] for h in range(heads)], axis=0
    )


def forward_kernel(heads, q_ref, key_value_ref, seg_ref, context_ref, probs_ref):
    slots, length = q_ref.shape[:2]
    row = lax.broadcasted_iota(jnp.int32, (length, length), 0)
    col = lax.broadcasted_iota(jnp.int32, (length, length), 1)
    for m in range(slots):
        seg = jnp.broadcast_to(seg_ref[m : m + 1, :].astype(F32), (length, length))
        allowed = (col <= row) & (seg == seg.T)
        q = stack_heads(q_ref[m], heads)
        scores = dot(q, key_value_ref[m, 0], NT) * (1.0 / math.sqrt(HEAD_SIZE))
        scores = scores.reshape(heads, length, length)
        masked = jnp.where(allowed[None], scores, -jnp.inf)
        expo = jnp.exp(masked - jnp.max(masked, axis=-1, keepdims=True))
        probs = expo / jnp.sum(expo, axis=-1, keepdims=True)
        probs = probs.reshape(heads * length, length)
        probs_ref[m] = probs
        context = dot(probs.astype(BF), key_value_ref[m, 1]).astype(BF)
        for h in range(heads):
            context_ref[m * length : (m + 1) * length, h * HEAD_SIZE : (h + 1) * HEAD_SIZE] = (
                context[h * length : (h + 1) * length]
            )


def backward_kernel(
    heads, own_ref, got_ref, q_ref, key_value_ref, probs_ref, query_grad_ref, key_value_grad_ref
):
    slots, length = q_ref.shape[:2]
    scale = 1.0 / math.sqrt(HEAD_SIZE)
    for m in range(slots):
        rows = slice(m * length, (m + 1) * length)
        grad = (own_ref[rows, :] + got_ref[rows, :].astype(F32)).astype(BF)
        grad = stack_heads(grad, heads)
        q = stack_heads(q_ref[m], heads)
        key, value = key_value_ref[m, 0], key_value_ref[m, 1]
        probs = probs_ref[m]
        prob_grad = dot(grad, value, NT)
        delta = jnp.sum(prob_grad * probs, axis=-1, keepdims=True)
        score_grad = probs * (prob_grad - delta)
        high = score_grad.astype(BF)
        low = (score_grad - high.astype(F32)).astype(BF)
        query_grad = ((dot(high, key) + dot(low, key)) * scale).astype(BF)
        for h in range(heads):
            query_grad_ref[m, :, h * HEAD_SIZE : (h + 1) * HEAD_SIZE] = query_grad[
                h * length : (h + 1) * length
            ]
        key_grad = (dot(high, q, TN) + dot(low, q, TN)) * scale
        key_value_grad_ref[m, 0] = key_grad.astype(BF)
        key_value_grad_ref[m, 1] = dot(probs.astype(BF), grad, TN).astype(BF)


def prepare_kernel(info_ref, cot_ref, out_ref, padded):
    slots, length, features = cot_ref.shape
    replicas = (info_ref.shape[0] - 2) // 2
    total = 0
    for r in range(2, 2 + replicas):
        total += info_ref[r] * info_ref[r + replicas]
    live = info_ref[2 + info_ref[0]]
    count = jnp.where(live > 0, info_ref[2 + replicas + info_ref[0]], 0)
    total = jnp.full((length, features), jnp.maximum(total, 1), jnp.int32).astype(F32)
    padded[:, features:] = jnp.zeros((slots * length, padded.shape[1] - features), F32)
    for m in range(slots):
        weight = jnp.where(jnp.full((length, features), m < count), 1.0, 0.0) / total
        padded[m * length : (m + 1) * length, :features] = cot_ref[m].astype(F32) * weight
    out_ref[...] = padded[...].T[:features].astype(BF)


def finish_kernel(kept_ref, got_ref, residual_ref, out_ref, padded):
    slots, length, features = residual_ref.shape
    padded[:features, :] = kept_ref[...].astype(F32) + got_ref[...].astype(F32)
    padded[features:, :] = jnp.zeros((padded.shape[0] - features, padded.shape[1]), F32)
    rows = padded[...].T
    for m in range(slots):
        out_ref[m] = (
            residual_ref[m].astype(F32) + rows[m * length : (m + 1) * length, :features]
        ).astype(BF)


def local_block(place_ref, mask, inner):
    core = place_ref[0] % 2
    index = (place_ref[1] % inner) ^ mask
    return ((index // (inner // 2)) ^ core) * (inner // 2) + index % (inner // 2)


def project_kernel(inner, place_ref, own_w, other_w, context_own, context_other, *refs):
    outs, total, turned = refs[:-2], refs[-2], refs[-1]
    step = pl.program_id(0)
    tokens = context_own.shape[0]
    features = own_w.shape[0]

    @pl.when(step == 0)
    def _():
        turned[:, :tokens] = context_own[...].T
        turned[:, tokens:] = context_other[...].T

    def rows(weight):
        at = pl.ds(pl.multiple_of(step * features, 16), features)
        total[at, :] = dot(weight, turned[...]).astype(BF)

    @pl.when(step < inner // 2)
    def _():
        rows(own_w[...])

    @pl.when(step >= inner // 2)
    def _():
        rows(other_w[...])

    @pl.when(step == inner - 1)
    def _():
        for mask in range(inner):
            at = pl.multiple_of(local_block(place_ref, mask, inner) * features, 16)
            block = total[pl.ds(at, features), :]
            outs[2 * mask][...] = block[:, :tokens]
            outs[2 * mask + 1][...] = block[:, tokens:]


def load_shards(inner, place_ref, shards, cot, first, sems):
    features, tokens = shards[0].shape
    copies = []
    for mask, shard in enumerate(shards):
        at = pl.multiple_of(local_block(place_ref, mask, inner) * features, 16)
        to = cot.at[pl.ds(at, features), pl.ds(first, tokens)]
        copies.append(pltpu.make_async_copy(shard, to, sems.at[first // tokens, mask]))
        copies[-1].start()
    return copies


def context_grad_kernel(inner, place_ref, own_w, other_w, *refs):
    shards, (out_ref, cot, turned, sems) = refs[:inner], refs[-4:]
    own_rows = own_w.shape[0]

    @pl.when(pl.program_id(0) == 0)
    def _():
        for copy in load_shards(inner, place_ref, shards, cot, 0, sems):
            copy.wait()
        turned[0] = cot[:own_rows, :].T
        turned[1] = cot[own_rows:, :].T

    total = dot(turned[0], own_w[...]) + dot(turned[1], other_w[...])
    out_ref[...] = total.astype(out_ref.dtype)


def weight_grad_kernel(inner, place_ref, context_own, context_other, *refs):
    shards, (own_ref, other_ref, cot, sems) = refs[: 2 * inner], refs[-4:]
    own_rows = own_ref.shape[0]
    tokens = context_own.shape[0]

    @pl.when(pl.program_id(0) == 0)
    def _():
        copies = load_shards(inner, place_ref, shards[:inner], cot, 0, sems)
        copies += load_shards(inner, place_ref, shards[inner:], cot, tokens, sems)
        for copy in copies:
            copy.wait()

    def rows(start):
        return dot(cot[start : start + own_rows, :tokens], context_own[...]) + dot(
            cot[start : start + own_rows, tokens:], context_other[...]
        )

    own_ref[...] = rows(0)
    other_ref[...] = rows(own_rows).astype(BF)


def place_kernel(place_ref, *refs):
    shards, (out_ref, sems) = refs[:-2], refs[-2:]
    copies = []
    for mask, shard in enumerate(shards):
        at = pl.multiple_of((place_ref[1] ^ mask) * HEAD_SIZE, HEAD_SIZE)
        copies.append(
            pltpu.make_async_copy(shard, out_ref.at[:, pl.ds(at, HEAD_SIZE)], sems.at[mask])
        )
    for copy in copies:
        copy.start()
    for copy in copies:
        copy.wait()


def by_activations(
    tensor_size,
    queries,
    slot_keys_values,
    segment_ids,
    residual_in,
    cotangent,
    out_weight,
    live_mask,
    micro_counts,
):
    inner = tensor_size // 2
    _, slots, length, width = queries.shape
    features = residual_in.shape[3]
    heads = width // HEAD_SIZE
    tokens = slots * length
    dp_idx, tensor_idx = lax.axis_index("dp"), lax.axis_index("tensor")
    place = jnp.stack([dp_idx, tensor_idx]).astype(jnp.int32)
    info = jnp.concatenate([place, live_mask, micro_counts])
    home = (dp_idx // 2) == (tensor_idx // inner)

    def swap(array, mask):
        return lax.ppermute(array, "tensor", [(t, t ^ mask) for t in range(tensor_size)])

    def swap_x(array):
        return lax.ppermute(array, "dp", [(d, d ^ 2) for d in range(4)])

    def swap_core(array):
        return lax.ppermute(array, "dp", [(d, d ^ 1) for d in range(4)])

    shape = jax.ShapeDtypeStruct
    wide = (features + 127) // 128 * 128

    scaled = call(
        prepare_kernel,
        shape((features, tokens), BF),
        [SMEM, pl.BlockSpec(cotangent.shape[1:])],
        0,
        4 * tokens * features,
        [pltpu.VMEM((tokens, wide), F32)],
    )(info, cotangent[0])
    across = swap(scaled, inner)

    weight_own = out_weight.T
    weight_other = swap_core(weight_own)
    own_rows = weight_own.shape[0]

    key_value = lax.dynamic_slice_in_dim(
        slot_keys_values[0], tensor_idx * HEAD_SIZE, HEAD_SIZE, axis=3
    )
    context, probs = call(
        functools.partial(forward_kernel, heads),
        (
            shape((tokens, width), BF),
            shape((slots, heads * length, length), F32),
        ),
        [pl.BlockSpec((slots, length, width)), pl.BlockSpec((slots, 2, length, HEAD_SIZE)), pl.BlockSpec((slots, length))],
        4 * tokens * width * length,
        4 * tokens * width * 2,
    )(queries[0], key_value, segment_ids[0])
    context_other = swap_x(context)
    across, context = lax.optimization_barrier((across, context))
    cot_own = jnp.where(home, scaled, across)
    cot_other = swap_x(jnp.where(home, across, scaled))
    shards_own = [swap(cot_own, mask) if mask else cot_own for mask in range(inner)]


    big = 2 * tokens * width * 2 * own_rows
    whole = lambda *dims: pl.BlockSpec(dims, lambda i: (0,) * len(dims))
    anywhere = pl.BlockSpec(memory_space=pl.ANY)
    half = inner // 2
    partial = call(
        functools.partial(project_kernel, inner),
        [shape((features, tokens), BF)] * (2 * inner),
        [
            SMEM,
            pl.BlockSpec((features, width), lambda i: (jnp.minimum(i, half - 1), 0)),
            pl.BlockSpec((features, width), lambda i: (jnp.maximum(i - half, 0), 0)),
            whole(tokens, width),
            whole(tokens, width),
        ],
        2 * big,
        4 * own_rows * width,
        [pltpu.VMEM((2 * own_rows, 2 * tokens), BF), pltpu.VMEM((width, 2 * tokens), BF)],
        out_specs=[whole(features, tokens)] * (2 * inner),
        grid=(inner,),
    )(place, weight_own, weight_other, context, context_other)
    cot_other, partial = lax.optimization_barrier((cot_other, partial))
    shards_other = [swap(cot_other, mask) if mask else cot_other for mask in range(inner)]
    near, far = list(partial[::2]), partial[1::2]
    far = [swap(far[mask], mask) if mask else far[mask] for mask in range(inner)]

    tile = min(256, width)
    column = lambda rows: pl.BlockSpec((rows, tile), lambda i: (0, i))

    def context_grad(shards, dtype):
        return call(
            functools.partial(context_grad_kernel, inner),
            shape((tokens, width), dtype),
            [SMEM, column(own_rows), column(own_rows)] + [anywhere] * len(shards),
            big,
            4 * own_rows * width,
            [
                pltpu.VMEM((2 * own_rows, tokens), BF),
                pltpu.VMEM((2, tokens, own_rows), BF),
                pltpu.SemaphoreType.DMA((1, inner)),
            ],
            out_specs=column(tokens),
            grid=(width // tile,),
        )(place, weight_own, weight_other, *shards)

    grad_own = context_grad(shards_own, F32)
    grad_other = context_grad(shards_other + [grad_own], BF)
    grad_got = swap_x(grad_other)

    *near, _ = lax.optimization_barrier((*near, grad_other))
    near = [swap(near[mask], mask) if mask else near[mask] for mask in range(inner)]
    add = lambda blocks: sum(block.astype(F32) for block in blocks).astype(BF)
    near_sum, far_sum = add(near), add(far)
    far_got = swap_x(far_sum)

    far_sum, context_late = lax.optimization_barrier((far_sum, context))
    weight_grad, weight_grad_other = call(
        functools.partial(weight_grad_kernel, inner),
        (
            shape((own_rows, width), F32),
            shape((own_rows, width), BF),
        ),
        [SMEM, column(tokens), column(tokens)] + [anywhere] * (2 * inner + 1),
        2 * big,
        6 * own_rows * width,
        [
            pltpu.VMEM((2 * own_rows, 2 * tokens), BF),
            pltpu.SemaphoreType.DMA((2, inner)),
        ],
        out_specs=(column(own_rows), column(own_rows)),
        grid=(width // tile,),
    )(place, context_late, context_other, *shards_own, *shards_other, grad_other)
    grad_got, weight_grad_other, near_sum = lax.optimization_barrier(
        (grad_got, weight_grad_other, near_sum)
    )
    query_gradient, key_value_part = call(
        functools.partial(backward_kernel, heads),
        (
            shape((slots, length, width), BF),
            shape((slots, 2, length, HEAD_SIZE), BF),
        ),
        [VMEM] * 5,
        14 * tokens * width * length,
        8 * tokens * width * 2,
    )(grad_own, grad_got, queries[0], key_value, probs)
    weight_grad = (weight_grad + swap_core(weight_grad_other).astype(F32)).T

    rows = slots * 2 * length
    part = key_value_part.reshape(rows, HEAD_SIZE)
    parts = [swap(part, mask) if mask else part for mask in range(inner)]
    far_got, _ = lax.optimization_barrier((far_got, part))
    part = swap(part, inner)
    kept = jnp.where(home, near_sum, far_got)
    got = swap(jnp.where(home, far_got, near_sum), inner)
    part, weight_grad = lax.optimization_barrier((part, weight_grad))
    parts += [swap(part, mask) if mask else part for mask in range(inner)]
    block_residual = call(
        finish_kernel,
        shape((slots, length, features), BF),
        [VMEM] * 3,
        0,
        8 * tokens * features,
        [pltpu.VMEM((wide, tokens), F32)],
    )(kept, got, residual_in[0])[None]
    key_value_gradient = call(
        place_kernel,
        shape((rows, KEY_VALUE_HEADS * HEAD_SIZE), BF),
        [SMEM] + [pl.BlockSpec(memory_space=pl.ANY)] * tensor_size,
        0,
        2 * rows * KEY_VALUE_HEADS * HEAD_SIZE,
        [pltpu.SemaphoreType.DMA((tensor_size,))],
        out_specs=pl.BlockSpec(memory_space=pl.ANY),
    )(place, *parts)
    key_value_gradient = key_value_gradient.reshape(
        1, slots, 2, length, KEY_VALUE_HEADS * HEAD_SIZE
    )
    return block_residual, query_gradient[None], key_value_gradient, weight_grad


def attention_backward(query_f, key_f, value_f, probs, rounded, grad_heads):
    prob_grad = jnp.einsum("mhqd,mhkd->mhqk", grad_heads, value_f, precision=lax.Precision.HIGHEST)
    delta = jnp.sum(prob_grad * probs, axis=-1, keepdims=True)
    score_grad = probs * (prob_grad - delta)
    query_gradient = jnp.einsum(
        "mhqk,mhkd->mhqd", score_grad, key_f, precision=lax.Precision.HIGHEST
    ) / math.sqrt(HEAD_SIZE)
    key_term = jnp.einsum(
        "mhqk,mhqd->mhkd", score_grad, query_f, precision=lax.Precision.HIGHEST
    ) / math.sqrt(HEAD_SIZE)
    value_term = jnp.einsum("mhqk,mhqd->mhkd", rounded, grad_heads, precision=lax.Precision.HIGHEST)
    return (query_gradient, key_term, value_term)


def by_weights(
    queries,
    slot_keys_values,
    segment_ids,
    residual_in,
    cotangent,
    out_weight,
    live_mask,
    micro_counts,
):
    tensor_size = lax.axis_size("tensor")
    heads_here = QUERY_HEADS // tensor_size
    heads_per_group = QUERY_HEADS // KEY_VALUE_HEADS
    tensor_idx = lax.axis_index("tensor")
    replica_idx = lax.axis_index("dp")
    query_here = queries[0]
    slot_total_count = query_here.shape[0]
    sequence_length = query_here.shape[1]
    local_feats = residual_in.shape[3]
    key_value_local = slot_keys_values[0].reshape(
        slot_total_count, 2, sequence_length, KEY_VALUE_HEADS, HEAD_SIZE
    )
    segments = segment_ids[0]
    head_ids = tensor_idx * heads_here + jnp.arange(heads_here)
    key_value_head_rows = head_ids // heads_per_group
    query_heads = query_here.reshape(
        slot_total_count, sequence_length, heads_here, HEAD_SIZE
    ).transpose(0, 2, 1, 3)
    key_head_rows = jnp.take(key_value_local[:, 0], key_value_head_rows, axis=2).transpose(
        0, 2, 1, 3
    )
    value_heads = jnp.take(key_value_local[:, 1], key_value_head_rows, axis=2).transpose(0, 2, 1, 3)
    positions = jnp.arange(sequence_length)
    allowed = (positions[None, :] <= positions[:, None])[None] & (
        segments[:, :, None] == segments[:, None, :]
    )
    allowed = allowed[:, None]
    scores = jnp.einsum(
        "mhqd,mhkd->mhqk", query_heads, key_head_rows, preferred_element_type=jnp.float32
    ) / math.sqrt(HEAD_SIZE)
    masked = jnp.where(allowed, scores, -jnp.inf)
    top_score = jnp.max(masked, axis=-1, keepdims=True)
    expo = jnp.where(allowed, jnp.exp(masked - top_score), 0.0)
    probs = expo / jnp.sum(expo, axis=-1, keepdims=True)
    probs_low = probs.astype(jnp.bfloat16)
    context = jnp.einsum(
        "mhqk,mhkd->mqhd", probs_low, value_heads, preferred_element_type=jnp.float32
    )
    context = context.astype(jnp.bfloat16).reshape(
        slot_total_count, sequence_length, heads_here * HEAD_SIZE
    )
    context_rows = context.reshape(slot_total_count * sequence_length, heads_here * HEAD_SIZE)
    weight_rows = lax.all_gather(out_weight, "dp", axis=1, tiled=True)
    reduced_total = lax.psum_scatter(
        jnp.einsum(
            "hd,nh->dn", weight_rows, context_rows, preferred_element_type=jnp.float32
        ).astype(jnp.bfloat16),
        "tensor",
        scatter_dimension=0,
        tiled=True,
    ).astype(jnp.float32)
    reduced_total = reduced_total.transpose(1, 0).reshape(
        slot_total_count, sequence_length, local_feats
    )
    block_residual = (residual_in[0].astype(jnp.float32) + reduced_total).astype(jnp.bfloat16)[None]
    replica_pick = jnp.arange(live_mask.shape[0]) == replica_idx
    my_live = jnp.sum(jnp.where(replica_pick, live_mask, 0))
    my_count = jnp.sum(jnp.where(replica_pick, micro_counts, 0))
    live_total = jnp.maximum(jnp.sum(live_mask * micro_counts), 1)
    slot_live = (jnp.arange(slot_total_count) < my_count) & (my_live > 0)
    slot_weight = slot_live.astype(jnp.float32) / live_total.astype(jnp.float32)
    scaled_cot = (cotangent[0].astype(jnp.float32) * slot_weight[:, None, None]).astype(
        jnp.bfloat16
    )
    weight_back = lax.all_gather(out_weight, "dp", axis=1, tiled=True)
    shard_piece = lax.all_gather(scaled_cot, "tensor", axis=2, tiled=True)
    grad_piece = jnp.einsum("msh,msd->hd", context, shard_piece, preferred_element_type=jnp.float32)
    grad_rows = grad_piece
    context_grad = jnp.einsum(
        "msd,hd->msh", shard_piece, weight_back, preferred_element_type=jnp.float32
    )
    grad_rows, context_grad = (grad_rows, context_grad)
    projection_weight_gradient = lax.psum_scatter(
        grad_rows.astype(jnp.bfloat16), "dp", scatter_dimension=1, tiled=True
    ).astype(jnp.float32)
    grad_heads = context_grad.reshape(
        slot_total_count, sequence_length, heads_here, HEAD_SIZE
    ).transpose(0, 2, 1, 3)
    query_f = query_heads.astype(jnp.float32)
    key_f = key_head_rows.astype(jnp.float32)
    value_f = value_heads.astype(jnp.float32)
    rounded = probs_low.astype(jnp.float32)
    query_gradient, key_term, value_term = attention_backward(
        query_f, key_f, value_f, probs, rounded, grad_heads
    )
    query_out = (
        query_gradient.transpose(0, 2, 1, 3)
        .reshape(slot_total_count, sequence_length, heads_here * HEAD_SIZE)
        .astype(jnp.bfloat16)[None]
    )
    addend_terms = (
        jnp.stack([key_term, value_term], axis=1).astype(jnp.bfloat16).astype(jnp.float32)
    )
    head_choice = (key_value_head_rows[:, None] == jnp.arange(KEY_VALUE_HEADS)[None, :]).astype(
        jnp.float32
    )
    positioned = jnp.einsum(
        "mchsd,hk->mcskd", addend_terms, head_choice, precision=lax.Precision.HIGHEST
    )
    positioned = positioned.reshape(
        slot_total_count, 2, sequence_length, KEY_VALUE_HEADS * HEAD_SIZE
    )
    keyval_sum = lax.psum(positioned.astype(jnp.bfloat16), "tensor")
    key_value_gradient = keyval_sum[None]
    return (block_residual, query_out, key_value_gradient, projection_weight_gradient)


def solution(mesh):
    dp_size, tensor_size = mesh.shape["dp"], mesh.shape["tensor"]
    regular = dp_size == 4 and tensor_size % 4 == 0 and tensor_size & (tensor_size - 1) == 0
    regular = regular and tensor_size == KEY_VALUE_HEADS
    per_device = functools.partial(by_activations, tensor_size) if regular else by_weights
    placed = (
        P("dp", None, None, "tensor"),
        P("dp", None, None, None, None),
        P("dp", None, None),
        P("dp", None, None, "tensor"),
        P("dp", None, None, "tensor"),
        P("tensor", "dp"),
        P(),
        P(),
    )
    return jax.shard_map(
        per_device,
        mesh=mesh,
        in_specs=placed,
        out_specs=(
            P("dp", None, None, "tensor"),
            P("dp", None, None, "tensor"),
            P("dp", None, None, None, None),
            P("tensor", "dp"),
        ),
        check_vma=False,
    )
```

```python
import functools
import math

import jax
import jax.numpy as jnp
from jax import lax
from jax.experimental import pallas as pl
from jax.experimental.pallas import tpu as pltpu
from jax.sharding import PartitionSpec as P

HEAD_SIZE = 128
QUERY_HEADS = 64
KEY_VALUE_HEADS = 8
BF = jnp.bfloat16
F32 = jnp.float32
VMEM = pl.BlockSpec(memory_space=pltpu.VMEM)
SMEM = pl.BlockSpec(memory_space=pltpu.SMEM)
NT = (((1,), (1,)), ((), ()))
TN = (((0,), (0,)), ((), ()))
NN = (((1,), (0,)), ((), ()))
LIMIT = 28 * 1024 * 1024


def dot(a, b, dims=NN):
    return lax.dot_general(a, b, dims, preferred_element_type=F32)


def call(kernel, out_shape, in_specs, flops, moved, scratch=(), **grid):
    return pl.pallas_call(
        kernel,
        out_shape=out_shape,
        in_specs=in_specs,
        scratch_shapes=scratch,
        cost_estimate=pl.CostEstimate(flops=flops, bytes_accessed=moved, transcendentals=0),
        compiler_params=pltpu.CompilerParams(vmem_limit_bytes=LIMIT),
        **grid,
    )


def stack_heads(rows, heads):
    return jnp.concatenate(
        [rows[:, h * HEAD_SIZE : (h + 1) * HEAD_SIZE] for h in range(heads)], axis=0
    )


def forward_kernel(heads, q_ref, key_value_ref, seg_ref, context_ref, probs_ref):
    slots, length = q_ref.shape[:2]
    row = lax.broadcasted_iota(jnp.int32, (length, length), 0)
    col = lax.broadcasted_iota(jnp.int32, (length, length), 1)
    for m in range(slots):
        seg = jnp.broadcast_to(seg_ref[m : m + 1, :].astype(F32), (length, length))
        allowed = (col <= row) & (seg == seg.T)
        q = stack_heads(q_ref[m], heads)
        scores = dot(q, key_value_ref[m, 0], NT) * (1.0 / math.sqrt(HEAD_SIZE))
        scores = scores.reshape(heads, length, length)
        masked = jnp.where(allowed[None], scores, -jnp.inf)
        expo = jnp.exp(masked - jnp.max(masked, axis=-1, keepdims=True))
        probs = expo / jnp.sum(expo, axis=-1, keepdims=True)
        probs = probs.reshape(heads * length, length)
        probs_ref[m] = probs
        context = dot(probs.astype(BF), key_value_ref[m, 1]).astype(BF)
        for h in range(heads):
            context_ref[m * length : (m + 1) * length, h * HEAD_SIZE : (h + 1) * HEAD_SIZE] = (
                context[h * length : (h + 1) * length]
            )


def backward_kernel(
    heads, own_ref, got_ref, q_ref, key_value_ref, probs_ref, query_grad_ref, key_value_grad_ref
):
    slots, length = q_ref.shape[:2]
    scale = 1.0 / math.sqrt(HEAD_SIZE)
    for m in range(slots):
        rows = slice(m * length, (m + 1) * length)
        grad = (own_ref[rows, :] + got_ref[rows, :].astype(F32)).astype(BF)
        grad = stack_heads(grad, heads)
        q = stack_heads(q_ref[m], heads)
        key, value = key_value_ref[m, 0], key_value_ref[m, 1]
        probs = probs_ref[m]
        prob_grad = dot(grad, value, NT)
        delta = jnp.sum(prob_grad * probs, axis=-1, keepdims=True)
        score_grad = probs * (prob_grad - delta)
        high = score_grad.astype(BF)
        low = (score_grad - high.astype(F32)).astype(BF)
        query_grad = ((dot(high, key) + dot(low, key)) * scale).astype(BF)
        for h in range(heads):
            query_grad_ref[m, :, h * HEAD_SIZE : (h + 1) * HEAD_SIZE] = query_grad[
                h * length : (h + 1) * length
            ]
        key_grad = (dot(high, q, TN) + dot(low, q, TN)) * scale
        key_value_grad_ref[m, 0] = key_grad.astype(BF)
        key_value_grad_ref[m, 1] = dot(probs.astype(BF), grad, TN).astype(BF)


def turn_kernel(cot_ref, out_ref, padded):
    slots, length, features = cot_ref.shape
    padded[:, features:] = jnp.zeros((slots * length, padded.shape[1] - features), F32)
    for m in range(slots):
        padded[m * length : (m + 1) * length, :features] = cot_ref[m].astype(F32)
    out_ref[...] = padded[...].T[:features].astype(BF)


def finish_kernel(kept_ref, got_ref, residual_ref, out_ref, padded):
    slots, length, features = residual_ref.shape
    padded[:features, :] = kept_ref[...].astype(F32) + got_ref[...].astype(F32)
    padded[features:, :] = jnp.zeros((padded.shape[0] - features, padded.shape[1]), F32)
    rows = padded[...].T
    for m in range(slots):
        out_ref[m] = (
            residual_ref[m].astype(F32) + rows[m * length : (m + 1) * length, :features]
        ).astype(BF)


def local_block(place_ref, mask, inner):
    core = place_ref[0] % 2
    index = (place_ref[1] % inner) ^ mask
    return ((index // (inner // 2)) ^ core) * (inner // 2) + index % (inner // 2)


def project_kernel(inner, place_ref, own_w, other_w, context_own, context_other, *refs):
    outs, total, turned = refs[:-2], refs[-2], refs[-1]
    step = pl.program_id(0)
    tokens = context_own.shape[0]
    features = own_w.shape[0]

    @pl.when(step == 0)
    def _():
        turned[:, :tokens] = context_own[...].T
        turned[:, tokens:] = context_other[...].T

    def rows(weight):
        at = pl.ds(pl.multiple_of(step * features, 16), features)
        total[at, :] = dot(weight, turned[...]).astype(BF)

    @pl.when(step < inner // 2)
    def _():
        rows(own_w[...])

    @pl.when(step >= inner // 2)
    def _():
        rows(other_w[...])

    @pl.when(step == inner - 1)
    def _():
        for mask in range(inner):
            at = pl.multiple_of(local_block(place_ref, mask, inner) * features, 16)
            block = total[pl.ds(at, features), :]
            outs[2 * mask][...] = block[:, :tokens]
            outs[2 * mask + 1][...] = block[:, tokens:]


def load_shards(inner, place_ref, shards, cot, first, sems):
    features, tokens = shards[0].shape
    copies = []
    for mask, shard in enumerate(shards):
        at = pl.multiple_of(local_block(place_ref, mask, inner) * features, 16)
        to = cot.at[pl.ds(at, features), pl.ds(first, tokens)]
        copies.append(pltpu.make_async_copy(shard, to, sems.at[first // tokens, mask]))
        copies[-1].start()
    return copies


def context_grad_kernel(inner, place_ref, own_w, other_w, *refs):
    shards, (out_ref, cot, turned, sems) = refs[:inner], refs[-4:]
    own_rows = own_w.shape[0]

    @pl.when(pl.program_id(0) == 0)
    def _():
        for copy in load_shards(inner, place_ref, shards, cot, 0, sems):
            copy.wait()
        turned[0] = cot[:own_rows, :].T
        turned[1] = cot[own_rows:, :].T

    total = dot(turned[0], own_w[...]) + dot(turned[1], other_w[...])
    out_ref[...] = total.astype(out_ref.dtype)


def weight_grad_kernel(inner, place_ref, context_own, context_other, *refs):
    shards, (own_ref, other_ref, cot, sems) = refs[: 2 * inner], refs[-4:]
    own_rows = own_ref.shape[0]
    tokens = context_own.shape[0]

    @pl.when(pl.program_id(0) == 0)
    def _():
        copies = load_shards(inner, place_ref, shards[:inner], cot, 0, sems)
        copies += load_shards(inner, place_ref, shards[inner:], cot, tokens, sems)
        for copy in copies:
            copy.wait()

    def rows(start):
        return dot(cot[start : start + own_rows, :tokens], context_own[...]) + dot(
            cot[start : start + own_rows, tokens:], context_other[...]
        )

    own_ref[...] = rows(0)
    other_ref[...] = rows(own_rows).astype(BF)


def place_kernel(place_ref, *refs):
    shards, (out_ref, sems) = refs[:-2], refs[-2:]
    copies = []
    for mask, shard in enumerate(shards):
        at = pl.multiple_of((place_ref[1] ^ mask) * HEAD_SIZE, HEAD_SIZE)
        copies.append(
            pltpu.make_async_copy(shard, out_ref.at[:, pl.ds(at, HEAD_SIZE)], sems.at[mask])
        )
    for copy in copies:
        copy.start()
    for copy in copies:
        copy.wait()


def slot_weights(live_mask, micro_counts, slots):
    replica = lax.axis_index("dp")
    pick = jnp.arange(live_mask.shape[0]) == replica
    my_live = jnp.sum(jnp.where(pick, live_mask, 0))
    my_count = jnp.sum(jnp.where(pick, micro_counts, 0))
    live_total = jnp.maximum(jnp.sum(live_mask * micro_counts), 1)
    slot_live = (jnp.arange(slots) < my_count) & (my_live > 0)
    return slot_live.astype(F32) / live_total.astype(F32)


def by_activations(
    tensor_size,
    queries,
    slot_keys_values,
    segment_ids,
    residual_in,
    cotangent,
    out_weight,
    live_mask,
    micro_counts,
):
    inner = tensor_size // 2
    _, slots, length, width = queries.shape
    features = residual_in.shape[3]
    heads = width // HEAD_SIZE
    tokens = slots * length
    dp_idx, tensor_idx = lax.axis_index("dp"), lax.axis_index("tensor")
    place = jnp.stack([dp_idx, tensor_idx]).astype(jnp.int32)
    home = (dp_idx // 2) == (tensor_idx // inner)

    def swap(array, mask):
        return lax.ppermute(array, "tensor", [(t, t ^ mask) for t in range(tensor_size)])

    def swap_x(array):
        return lax.ppermute(array, "dp", [(d, d ^ 2) for d in range(4)])

    def swap_core(array):
        return lax.ppermute(array, "dp", [(d, d ^ 1) for d in range(4)])

    shape = jax.ShapeDtypeStruct
    wide = (features + 127) // 128 * 128

    turned = call(
        turn_kernel,
        shape((features, tokens), BF),
        [pl.BlockSpec(cotangent.shape[1:])],
        0,
        4 * tokens * features,
        [pltpu.VMEM((tokens, wide), F32)],
    )(cotangent[0])
    across = swap(turned, inner)

    weight_own = out_weight.T
    weight_other = swap_core(weight_own)
    own_rows = weight_own.shape[0]

    key_value = lax.dynamic_slice_in_dim(
        slot_keys_values[0], tensor_idx * HEAD_SIZE, HEAD_SIZE, axis=3
    )
    context, probs = call(
        functools.partial(forward_kernel, heads),
        (
            shape((tokens, width), BF),
            shape((slots, heads * length, length), F32),
        ),
        [pl.BlockSpec((slots, length, width)), pl.BlockSpec((slots, 2, length, HEAD_SIZE)), pl.BlockSpec((slots, length))],
        4 * tokens * width * length,
        4 * tokens * width * 2,
    )(queries[0], key_value, segment_ids[0])
    context_other = swap_x(context)
    across, context = lax.optimization_barrier((across, context))
    weight = jnp.repeat(slot_weights(live_mask, micro_counts, slots), length)
    scaled = lambda array: (array.astype(F32) * weight[None, :]).astype(BF)
    cot_own = scaled(jnp.where(home, turned, across))
    cot_other = swap_x(scaled(jnp.where(home, across, turned)))
    shards_own = [swap(cot_own, mask) if mask else cot_own for mask in range(inner)]


    cot_other, context_other = lax.optimization_barrier((cot_other, context_other))

    big = 2 * tokens * width * 2 * own_rows
    whole = lambda *dims: pl.BlockSpec(dims, lambda i: (0,) * len(dims))
    anywhere = pl.BlockSpec(memory_space=pl.ANY)
    half = inner // 2
    partial = call(
        functools.partial(project_kernel, inner),
        [shape((features, tokens), BF)] * (2 * inner),
        [
            SMEM,
            pl.BlockSpec((features, width), lambda i: (jnp.minimum(i, half - 1), 0)),
            pl.BlockSpec((features, width), lambda i: (jnp.maximum(i - half, 0), 0)),
            whole(tokens, width),
            whole(tokens, width),
        ],
        2 * big,
        4 * own_rows * width,
        [pltpu.VMEM((2 * own_rows, 2 * tokens), BF), pltpu.VMEM((width, 2 * tokens), BF)],
        out_specs=[whole(features, tokens)] * (2 * inner),
        grid=(inner,),
    )(place, weight_own, weight_other, context, context_other)
    shards_other = [swap(cot_other, mask) if mask else cot_other for mask in range(inner)]
    near, far = list(partial[::2]), partial[1::2]
    far = [swap(far[mask], mask) if mask else far[mask] for mask in range(inner)]

    tile = min(256, width)
    column = lambda rows: pl.BlockSpec((rows, tile), lambda i: (0, i))

    def context_grad(shards, dtype):
        return call(
            functools.partial(context_grad_kernel, inner),
            shape((tokens, width), dtype),
            [SMEM, column(own_rows), column(own_rows)] + [anywhere] * len(shards),
            big,
            4 * own_rows * width,
            [
                pltpu.VMEM((2 * own_rows, tokens), BF),
                pltpu.VMEM((2, tokens, own_rows), BF),
                pltpu.SemaphoreType.DMA((1, inner)),
            ],
            out_specs=column(tokens),
            grid=(width // tile,),
        )(place, weight_own, weight_other, *shards)

    grad_own = context_grad(shards_own, F32)
    grad_other = context_grad(shards_other + [grad_own], BF)
    grad_got = swap_x(grad_other)

    *near, _ = lax.optimization_barrier((*near, grad_other))
    near = [swap(near[mask], mask) if mask else near[mask] for mask in range(inner)]
    add = lambda blocks: sum(block.astype(F32) for block in blocks).astype(BF)
    near_sum, far_sum = add(near), add(far)
    far_got = swap_x(far_sum)

    far_sum, context_late = lax.optimization_barrier((far_sum, context))
    weight_grad, weight_grad_other = call(
        functools.partial(weight_grad_kernel, inner),
        (
            shape((own_rows, width), F32),
            shape((own_rows, width), BF),
        ),
        [SMEM, column(tokens), column(tokens)] + [anywhere] * (2 * inner + 1),
        2 * big,
        6 * own_rows * width,
        [
            pltpu.VMEM((2 * own_rows, 2 * tokens), BF),
            pltpu.SemaphoreType.DMA((2, inner)),
        ],
        out_specs=(column(own_rows), column(own_rows)),
        grid=(width // tile,),
    )(place, context_late, context_other, *shards_own, *shards_other, grad_other)
    grad_got, weight_grad_other, near_sum, far_got = lax.optimization_barrier(
        (grad_got, weight_grad_other, near_sum, far_got)
    )
    query_gradient, key_value_part = call(
        functools.partial(backward_kernel, heads),
        (
            shape((slots, length, width), BF),
            shape((slots, 2, length, HEAD_SIZE), BF),
        ),
        [VMEM] * 5,
        14 * tokens * width * length,
        8 * tokens * width * 2,
    )(grad_own, grad_got, queries[0], key_value, probs)
    weight_grad = (weight_grad + swap_core(weight_grad_other).astype(F32)).T

    rows = slots * 2 * length
    part = key_value_part.reshape(rows, HEAD_SIZE)
    parts = [swap(part, mask) if mask else part for mask in range(inner)]
    part = swap(part, inner)
    part, weight_grad = lax.optimization_barrier((part, weight_grad))
    parts += [swap(part, mask) if mask else part for mask in range(inner)]
    kept = jnp.where(home, near_sum, far_got)
    got = swap(jnp.where(home, far_got, near_sum), inner)
    got, parts[1], parts[2], parts[3] = lax.optimization_barrier((got, parts[1], parts[2], parts[3]))
    block_residual = call(
        finish_kernel,
        shape((slots, length, features), BF),
        [VMEM] * 3,
        0,
        8 * tokens * features,
        [pltpu.VMEM((wide, tokens), F32)],
    )(kept, got, residual_in[0])[None]
    key_value_gradient = call(
        place_kernel,
        shape((rows, KEY_VALUE_HEADS * HEAD_SIZE), BF),
        [SMEM] + [pl.BlockSpec(memory_space=pl.ANY)] * tensor_size,
        0,
        2 * rows * KEY_VALUE_HEADS * HEAD_SIZE,
        [pltpu.SemaphoreType.DMA((tensor_size,))],
        out_specs=pl.BlockSpec(memory_space=pl.ANY),
    )(place, *parts)
    key_value_gradient = key_value_gradient.reshape(
        1, slots, 2, length, KEY_VALUE_HEADS * HEAD_SIZE
    )
    return block_residual, query_gradient[None], key_value_gradient, weight_grad


def attention_backward(query_f, key_f, value_f, probs, rounded, grad_heads):
    prob_grad = jnp.einsum("mhqd,mhkd->mhqk", grad_heads, value_f, precision=lax.Precision.HIGHEST)
    delta = jnp.sum(prob_grad * probs, axis=-1, keepdims=True)
    score_grad = probs * (prob_grad - delta)
    query_gradient = jnp.einsum(
        "mhqk,mhkd->mhqd", score_grad, key_f, precision=lax.Precision.HIGHEST
    ) / math.sqrt(HEAD_SIZE)
    key_term = jnp.einsum(
        "mhqk,mhqd->mhkd", score_grad, query_f, precision=lax.Precision.HIGHEST
    ) / math.sqrt(HEAD_SIZE)
    value_term = jnp.einsum("mhqk,mhqd->mhkd", rounded, grad_heads, precision=lax.Precision.HIGHEST)
    return (query_gradient, key_term, value_term)


def by_weights(
    queries,
    slot_keys_values,
    segment_ids,
    residual_in,
    cotangent,
    out_weight,
    live_mask,
    micro_counts,
):
    tensor_size = lax.axis_size("tensor")
    heads_here = QUERY_HEADS // tensor_size
    heads_per_group = QUERY_HEADS // KEY_VALUE_HEADS
    tensor_idx = lax.axis_index("tensor")
    replica_idx = lax.axis_index("dp")
    query_here = queries[0]
    slot_total_count = query_here.shape[0]
    sequence_length = query_here.shape[1]
    local_feats = residual_in.shape[3]
    key_value_local = slot_keys_values[0].reshape(
        slot_total_count, 2, sequence_length, KEY_VALUE_HEADS, HEAD_SIZE
    )
    segments = segment_ids[0]
    head_ids = tensor_idx * heads_here + jnp.arange(heads_here)
    key_value_head_rows = head_ids // heads_per_group
    query_heads = query_here.reshape(
        slot_total_count, sequence_length, heads_here, HEAD_SIZE
    ).transpose(0, 2, 1, 3)
    key_head_rows = jnp.take(key_value_local[:, 0], key_value_head_rows, axis=2).transpose(
        0, 2, 1, 3
    )
    value_heads = jnp.take(key_value_local[:, 1], key_value_head_rows, axis=2).transpose(0, 2, 1, 3)
    positions = jnp.arange(sequence_length)
    allowed = (positions[None, :] <= positions[:, None])[None] & (
        segments[:, :, None] == segments[:, None, :]
    )
    allowed = allowed[:, None]
    scores = jnp.einsum(
        "mhqd,mhkd->mhqk", query_heads, key_head_rows, preferred_element_type=jnp.float32
    ) / math.sqrt(HEAD_SIZE)
    masked = jnp.where(allowed, scores, -jnp.inf)
    top_score = jnp.max(masked, axis=-1, keepdims=True)
    expo = jnp.where(allowed, jnp.exp(masked - top_score), 0.0)
    probs = expo / jnp.sum(expo, axis=-1, keepdims=True)
    probs_low = probs.astype(jnp.bfloat16)
    context = jnp.einsum(
        "mhqk,mhkd->mqhd", probs_low, value_heads, preferred_element_type=jnp.float32
    )
    context = context.astype(jnp.bfloat16).reshape(
        slot_total_count, sequence_length, heads_here * HEAD_SIZE
    )
    context_rows = context.reshape(slot_total_count * sequence_length, heads_here * HEAD_SIZE)
    weight_rows = lax.all_gather(out_weight, "dp", axis=1, tiled=True)
    reduced_total = lax.psum_scatter(
        jnp.einsum(
            "hd,nh->dn", weight_rows, context_rows, preferred_element_type=jnp.float32
        ).astype(jnp.bfloat16),
        "tensor",
        scatter_dimension=0,
        tiled=True,
    ).astype(jnp.float32)
    reduced_total = reduced_total.transpose(1, 0).reshape(
        slot_total_count, sequence_length, local_feats
    )
    block_residual = (residual_in[0].astype(jnp.float32) + reduced_total).astype(jnp.bfloat16)[None]
    replica_pick = jnp.arange(live_mask.shape[0]) == replica_idx
    my_live = jnp.sum(jnp.where(replica_pick, live_mask, 0))
    my_count = jnp.sum(jnp.where(replica_pick, micro_counts, 0))
    live_total = jnp.maximum(jnp.sum(live_mask * micro_counts), 1)
    slot_live = (jnp.arange(slot_total_count) < my_count) & (my_live > 0)
    slot_weight = slot_live.astype(jnp.float32) / live_total.astype(jnp.float32)
    scaled_cot = (cotangent[0].astype(jnp.float32) * slot_weight[:, None, None]).astype(
        jnp.bfloat16
    )
    weight_back = lax.all_gather(out_weight, "dp", axis=1, tiled=True)
    shard_piece = lax.all_gather(scaled_cot, "tensor", axis=2, tiled=True)
    grad_piece = jnp.einsum("msh,msd->hd", context, shard_piece, preferred_element_type=jnp.float32)
    grad_rows = grad_piece
    context_grad = jnp.einsum(
        "msd,hd->msh", shard_piece, weight_back, preferred_element_type=jnp.float32
    )
    grad_rows, context_grad = (grad_rows, context_grad)
    projection_weight_gradient = lax.psum_scatter(
        grad_rows.astype(jnp.bfloat16), "dp", scatter_dimension=1, tiled=True
    ).astype(jnp.float32)
    grad_heads = context_grad.reshape(
        slot_total_count, sequence_length, heads_here, HEAD_SIZE
    ).transpose(0, 2, 1, 3)
    query_f = query_heads.astype(jnp.float32)
    key_f = key_head_rows.astype(jnp.float32)
    value_f = value_heads.astype(jnp.float32)
    rounded = probs_low.astype(jnp.float32)
    query_gradient, key_term, value_term = attention_backward(
        query_f, key_f, value_f, probs, rounded, grad_heads
    )
    query_out = (
        query_gradient.transpose(0, 2, 1, 3)
        .reshape(slot_total_count, sequence_length, heads_here * HEAD_SIZE)
        .astype(jnp.bfloat16)[None]
    )
    addend_terms = (
        jnp.stack([key_term, value_term], axis=1).astype(jnp.bfloat16).astype(jnp.float32)
    )
    head_choice = (key_value_head_rows[:, None] == jnp.arange(KEY_VALUE_HEADS)[None, :]).astype(
        jnp.float32
    )
    positioned = jnp.einsum(
        "mchsd,hk->mcskd", addend_terms, head_choice, precision=lax.Precision.HIGHEST
    )
    positioned = positioned.reshape(
        slot_total_count, 2, sequence_length, KEY_VALUE_HEADS * HEAD_SIZE
    )
    keyval_sum = lax.psum(positioned.astype(jnp.bfloat16), "tensor")
    key_value_gradient = keyval_sum[None]
    return (block_residual, query_out, key_value_gradient, projection_weight_gradient)


def solution(mesh):
    dp_size, tensor_size = mesh.shape["dp"], mesh.shape["tensor"]
    regular = dp_size == 4 and tensor_size % 4 == 0 and tensor_size & (tensor_size - 1) == 0
    regular = regular and tensor_size == KEY_VALUE_HEADS
    per_device = functools.partial(by_activations, tensor_size) if regular else by_weights
    placed = (
        P("dp", None, None, "tensor"),
        P("dp", None, None, None, None),
        P("dp", None, None),
        P("dp", None, None, "tensor"),
        P("dp", None, None, "tensor"),
        P("tensor", "dp"),
        P(),
        P(),
    )
    return jax.shard_map(
        per_device,
        mesh=mesh,
        in_specs=placed,
        out_specs=(
            P("dp", None, None, "tensor"),
            P("dp", None, None, "tensor"),
            P("dp", None, None, None, None),
            P("tensor", "dp"),
        ),
        check_vma=False,
    )
```

```python
import functools
import math

import jax
import jax.numpy as jnp
from jax import lax
from jax.experimental import pallas as pl
from jax.experimental.pallas import tpu as pltpu
from jax.sharding import PartitionSpec as P

HEAD_SIZE = 128
QUERY_HEADS = 64
KEY_VALUE_HEADS = 8
BF = jnp.bfloat16
F32 = jnp.float32
VMEM = pl.BlockSpec(memory_space=pltpu.VMEM)
SMEM = pl.BlockSpec(memory_space=pltpu.SMEM)
NT = (((1,), (1,)), ((), ()))
TN = (((0,), (0,)), ((), ()))
NN = (((1,), (0,)), ((), ()))
LIMIT = 28 * 1024 * 1024


def dot(a, b, dims=NN):
    return lax.dot_general(a, b, dims, preferred_element_type=F32)


def call(kernel, out_shape, in_specs, flops, moved, scratch=(), **grid):
    return pl.pallas_call(
        kernel,
        out_shape=out_shape,
        in_specs=in_specs,
        scratch_shapes=scratch,
        cost_estimate=pl.CostEstimate(flops=flops, bytes_accessed=moved, transcendentals=0),
        compiler_params=pltpu.CompilerParams(vmem_limit_bytes=LIMIT),
        **grid,
    )


def stack_heads(rows, heads):
    return jnp.concatenate(
        [rows[:, h * HEAD_SIZE : (h + 1) * HEAD_SIZE] for h in range(heads)], axis=0
    )


def forward_kernel(heads, q_ref, key_value_ref, seg_ref, context_ref, probs_ref):
    slots, length = q_ref.shape[:2]
    row = lax.broadcasted_iota(jnp.int32, (length, length), 0)
    col = lax.broadcasted_iota(jnp.int32, (length, length), 1)
    for m in range(slots):
        seg = jnp.broadcast_to(seg_ref[m : m + 1, :].astype(F32), (length, length))
        allowed = (col <= row) & (seg == seg.T)
        q = stack_heads(q_ref[m], heads)
        scores = dot(q, key_value_ref[m, 0], NT) * (1.0 / math.sqrt(HEAD_SIZE))
        scores = scores.reshape(heads, length, length)
        masked = jnp.where(allowed[None], scores, -jnp.inf)
        expo = jnp.exp(masked - jnp.max(masked, axis=-1, keepdims=True))
        probs = expo / jnp.sum(expo, axis=-1, keepdims=True)
        probs = probs.reshape(heads * length, length)
        probs_ref[m] = probs
        context = dot(probs.astype(BF), key_value_ref[m, 1]).astype(BF)
        for h in range(heads):
            context_ref[m * length : (m + 1) * length, h * HEAD_SIZE : (h + 1) * HEAD_SIZE] = (
                context[h * length : (h + 1) * length]
            )


def backward_kernel(
    heads, own_ref, got_ref, q_ref, key_value_ref, probs_ref, query_grad_ref, key_value_grad_ref
):
    slots, length = q_ref.shape[:2]
    scale = 1.0 / math.sqrt(HEAD_SIZE)
    for m in range(slots):
        rows = slice(m * length, (m + 1) * length)
        grad = (own_ref[rows, :] + got_ref[rows, :].astype(F32)).astype(BF)
        grad = stack_heads(grad, heads)
        q = stack_heads(q_ref[m], heads)
        key, value = key_value_ref[m, 0], key_value_ref[m, 1]
        probs = probs_ref[m]
        prob_grad = dot(grad, value, NT)
        delta = jnp.sum(prob_grad * probs, axis=-1, keepdims=True)
        score_grad = probs * (prob_grad - delta)
        high = score_grad.astype(BF)
        low = (score_grad - high.astype(F32)).astype(BF)
        query_grad = ((dot(high, key) + dot(low, key)) * scale).astype(BF)
        for h in range(heads):
            query_grad_ref[m, :, h * HEAD_SIZE : (h + 1) * HEAD_SIZE] = query_grad[
                h * length : (h + 1) * length
            ]
        key_grad = (dot(high, q, TN) + dot(low, q, TN)) * scale
        key_value_grad_ref[m, 0] = key_grad.astype(BF)
        key_value_grad_ref[m, 1] = dot(probs.astype(BF), grad, TN).astype(BF)


def turn_kernel(cot_ref, out_ref, padded):
    slots, length, features = cot_ref.shape
    padded[:, features:] = jnp.zeros((slots * length, padded.shape[1] - features), F32)
    for m in range(slots):
        padded[m * length : (m + 1) * length, :features] = cot_ref[m].astype(F32)
    out_ref[...] = padded[...].T[:features].astype(BF)


def finish_kernel(kept_ref, got_ref, residual_ref, out_ref, padded):
    slots, length, features = residual_ref.shape
    padded[:features, :] = kept_ref[...].astype(F32) + got_ref[...].astype(F32)
    padded[features:, :] = jnp.zeros((padded.shape[0] - features, padded.shape[1]), F32)
    rows = padded[...].T
    for m in range(slots):
        out_ref[m] = (
            residual_ref[m].astype(F32) + rows[m * length : (m + 1) * length, :features]
        ).astype(BF)


def local_block(place_ref, mask, inner):
    core = place_ref[0] % 2
    index = (place_ref[1] % inner) ^ mask
    return ((index // (inner // 2)) ^ core) * (inner // 2) + index % (inner // 2)


def project_kernel(inner, place_ref, own_w, other_w, context_own, context_other, *refs):
    outs, total, turned = refs[:-2], refs[-2], refs[-1]
    step = pl.program_id(0)
    tokens = context_own.shape[0]
    features = own_w.shape[0]

    @pl.when(step == 0)
    def _():
        turned[:, :tokens] = context_own[...].T
        turned[:, tokens:] = context_other[...].T

    def rows(weight):
        at = pl.ds(pl.multiple_of(step * features, 16), features)
        total[at, :] = dot(weight, turned[...]).astype(BF)

    @pl.when(step < inner // 2)
    def _():
        rows(own_w[...])

    @pl.when(step >= inner // 2)
    def _():
        rows(other_w[...])

    @pl.when(step == inner - 1)
    def _():
        for mask in range(inner):
            at = pl.multiple_of(local_block(place_ref, mask, inner) * features, 16)
            block = total[pl.ds(at, features), :]
            outs[2 * mask][...] = block[:, :tokens]
            outs[2 * mask + 1][...] = block[:, tokens:]


def load_shards(inner, place_ref, shards, cot, first, sems):
    features, tokens = shards[0].shape
    copies = []
    for mask, shard in enumerate(shards):
        at = pl.multiple_of(local_block(place_ref, mask, inner) * features, 16)
        to = cot.at[pl.ds(at, features), pl.ds(first, tokens)]
        copies.append(pltpu.make_async_copy(shard, to, sems.at[first // tokens, mask]))
        copies[-1].start()
    return copies


def context_grad_kernel(inner, place_ref, own_w, other_w, *refs):
    shards, (out_ref, cot, turned, sems) = refs[:inner], refs[-4:]
    own_rows = own_w.shape[0]

    @pl.when(pl.program_id(0) == 0)
    def _():
        for copy in load_shards(inner, place_ref, shards, cot, 0, sems):
            copy.wait()
        turned[0] = cot[:own_rows, :].T
        turned[1] = cot[own_rows:, :].T

    total = dot(turned[0], own_w[...]) + dot(turned[1], other_w[...])
    out_ref[...] = total.astype(out_ref.dtype)


def weight_grad_kernel(inner, place_ref, context_own, context_other, *refs):
    shards, (own_ref, other_ref, cot, sems) = refs[: 2 * inner], refs[-4:]
    own_rows = own_ref.shape[0]
    tokens = context_own.shape[0]

    @pl.when(pl.program_id(0) == 0)
    def _():
        copies = load_shards(inner, place_ref, shards[:inner], cot, 0, sems)
        copies += load_shards(inner, place_ref, shards[inner:], cot, tokens, sems)
        for copy in copies:
            copy.wait()

    def rows(start):
        return dot(cot[start : start + own_rows, :tokens], context_own[...]) + dot(
            cot[start : start + own_rows, tokens:], context_other[...]
        )

    own_ref[...] = rows(0)
    other_ref[...] = rows(own_rows).astype(BF)


def place_kernel(place_ref, *refs):
    shards, (out_ref, sems) = refs[:-2], refs[-2:]
    copies = []
    for mask, shard in enumerate(shards):
        at = pl.multiple_of((place_ref[1] ^ mask) * HEAD_SIZE, HEAD_SIZE)
        copies.append(
            pltpu.make_async_copy(shard, out_ref.at[:, pl.ds(at, HEAD_SIZE)], sems.at[mask])
        )
    for copy in copies:
        copy.start()
    for copy in copies:
        copy.wait()


def slot_weights(live_mask, micro_counts, slots):
    replica = lax.axis_index("dp")
    pick = jnp.arange(live_mask.shape[0]) == replica
    my_live = jnp.sum(jnp.where(pick, live_mask, 0))
    my_count = jnp.sum(jnp.where(pick, micro_counts, 0))
    live_total = jnp.maximum(jnp.sum(live_mask * micro_counts), 1)
    slot_live = (jnp.arange(slots) < my_count) & (my_live > 0)
    return slot_live.astype(F32) / live_total.astype(F32)


def by_activations(
    tensor_size,
    queries,
    slot_keys_values,
    segment_ids,
    residual_in,
    cotangent,
    out_weight,
    live_mask,
    micro_counts,
):
    inner = tensor_size // 2
    _, slots, length, width = queries.shape
    features = residual_in.shape[3]
    heads = width // HEAD_SIZE
    tokens = slots * length
    dp_idx, tensor_idx = lax.axis_index("dp"), lax.axis_index("tensor")
    place = jnp.stack([dp_idx, tensor_idx]).astype(jnp.int32)
    home = (dp_idx // 2) == (tensor_idx // inner)

    def swap(array, mask):
        return lax.ppermute(array, "tensor", [(t, t ^ mask) for t in range(tensor_size)])

    def swap_x(array):
        return lax.ppermute(array, "dp", [(d, d ^ 2) for d in range(4)])

    def swap_core(array):
        return lax.ppermute(array, "dp", [(d, d ^ 1) for d in range(4)])

    shape = jax.ShapeDtypeStruct
    wide = (features + 127) // 128 * 128

    turned = call(
        turn_kernel,
        shape((features, tokens), BF),
        [pl.BlockSpec(cotangent.shape[1:])],
        0,
        4 * tokens * features,
        [pltpu.VMEM((tokens, wide), F32)],
    )(cotangent[0])
    across = swap(turned, inner)

    weight_own = out_weight.T
    weight_other = swap_core(weight_own)
    own_rows = weight_own.shape[0]

    key_value = lax.dynamic_slice_in_dim(
        slot_keys_values[0], tensor_idx * HEAD_SIZE, HEAD_SIZE, axis=3
    )
    context, probs = call(
        functools.partial(forward_kernel, heads),
        (
            shape((tokens, width), BF),
            shape((slots, heads * length, length), F32),
        ),
        [pl.BlockSpec((slots, length, width)), pl.BlockSpec((slots, 2, length, HEAD_SIZE)), pl.BlockSpec((slots, length))],
        4 * tokens * width * length,
        4 * tokens * width * 2,
    )(queries[0], key_value, segment_ids[0])
    context_other = swap_x(context)
    across, context = lax.optimization_barrier((across, context))
    weight = jnp.repeat(slot_weights(live_mask, micro_counts, slots), length)
    scaled = lambda array: (array.astype(F32) * weight[None, :]).astype(BF)
    sent = scaled(jnp.where(home, across, turned))
    cot_other = swap_x(sent)
    across, _ = lax.optimization_barrier((across, sent))
    cot_own = scaled(jnp.where(home, turned, across))
    shards_own = [swap(cot_own, mask) if mask else cot_own for mask in range(inner)]


    cot_other, context_other = lax.optimization_barrier((cot_other, context_other))

    big = 2 * tokens * width * 2 * own_rows
    whole = lambda *dims: pl.BlockSpec(dims, lambda i: (0,) * len(dims))
    anywhere = pl.BlockSpec(memory_space=pl.ANY)
    half = inner // 2
    partial = call(
        functools.partial(project_kernel, inner),
        [shape((features, tokens), BF)] * (2 * inner),
        [
            SMEM,
            pl.BlockSpec((features, width), lambda i: (jnp.minimum(i, half - 1), 0)),
            pl.BlockSpec((features, width), lambda i: (jnp.maximum(i - half, 0), 0)),
            whole(tokens, width),
            whole(tokens, width),
        ],
        2 * big,
        4 * own_rows * width,
        [pltpu.VMEM((2 * own_rows, 2 * tokens), BF), pltpu.VMEM((width, 2 * tokens), BF)],
        out_specs=[whole(features, tokens)] * (2 * inner),
        grid=(inner,),
    )(place, weight_own, weight_other, context, context_other)
    shards_other = [swap(cot_other, mask) if mask else cot_other for mask in range(inner)]
    near, far = list(partial[::2]), partial[1::2]
    far = [swap(far[mask], mask) if mask else far[mask] for mask in range(inner)]

    tile = min(512, width)
    column = lambda rows: pl.BlockSpec((rows, tile), lambda i: (0, i))

    def context_grad(shards, dtype):
        return call(
            functools.partial(context_grad_kernel, inner),
            shape((tokens, width), dtype),
            [SMEM, column(own_rows), column(own_rows)] + [anywhere] * len(shards),
            big,
            4 * own_rows * width,
            [
                pltpu.VMEM((2 * own_rows, tokens), BF),
                pltpu.VMEM((2, tokens, own_rows), BF),
                pltpu.SemaphoreType.DMA((1, inner)),
            ],
            out_specs=column(tokens),
            grid=(width // tile,),
        )(place, weight_own, weight_other, *shards)

    grad_own = context_grad(shards_own, F32)
    grad_other = context_grad(shards_other + [grad_own], BF)
    grad_got = swap_x(grad_other)

    *near, _ = lax.optimization_barrier((*near, grad_other))
    near = [swap(near[mask], mask) if mask else near[mask] for mask in range(inner)]
    add = lambda blocks: sum(block.astype(F32) for block in blocks).astype(BF)
    near_sum, far_sum = add(near), add(far)
    far_got = swap_x(far_sum)

    far_sum, context_late = lax.optimization_barrier((far_sum, context))
    weight_grad, weight_grad_other = call(
        functools.partial(weight_grad_kernel, inner),
        (
            shape((own_rows, width), F32),
            shape((own_rows, width), BF),
        ),
        [SMEM, column(tokens), column(tokens)] + [anywhere] * (2 * inner + 1),
        2 * big,
        6 * own_rows * width,
        [
            pltpu.VMEM((2 * own_rows, 2 * tokens), BF),
            pltpu.SemaphoreType.DMA((2, inner)),
        ],
        out_specs=(column(own_rows), column(own_rows)),
        grid=(width // tile,),
    )(place, context_late, context_other, *shards_own, *shards_other, grad_other)
    grad_got, weight_grad_other, near_sum, far_got = lax.optimization_barrier(
        (grad_got, weight_grad_other, near_sum, far_got)
    )
    query_gradient, key_value_part = call(
        functools.partial(backward_kernel, heads),
        (
            shape((slots, length, width), BF),
            shape((slots, 2, length, HEAD_SIZE), BF),
        ),
        [VMEM] * 5,
        14 * tokens * width * length,
        8 * tokens * width * 2,
    )(grad_own, grad_got, queries[0], key_value, probs)
    weight_grad = (weight_grad + swap_core(weight_grad_other).astype(F32)).T

    rows = slots * 2 * length
    part = key_value_part.reshape(rows, HEAD_SIZE)
    parts = [swap(part, mask) if mask else part for mask in range(inner)]
    part = swap(part, inner)
    part, weight_grad = lax.optimization_barrier((part, weight_grad))
    parts += [swap(part, mask) if mask else part for mask in range(inner)]
    kept = jnp.where(home, near_sum, far_got)
    got = swap(jnp.where(home, far_got, near_sum), inner)
    got, parts[1], parts[2], parts[3] = lax.optimization_barrier((got, parts[1], parts[2], parts[3]))
    block_residual = call(
        finish_kernel,
        shape((slots, length, features), BF),
        [VMEM] * 3,
        0,
        8 * tokens * features,
        [pltpu.VMEM((wide, tokens), F32)],
    )(kept, got, residual_in[0])[None]
    key_value_gradient = call(
        place_kernel,
        shape((rows, KEY_VALUE_HEADS * HEAD_SIZE), BF),
        [SMEM] + [pl.BlockSpec(memory_space=pl.ANY)] * tensor_size,
        0,
        2 * rows * KEY_VALUE_HEADS * HEAD_SIZE,
        [pltpu.SemaphoreType.DMA((tensor_size,))],
        out_specs=pl.BlockSpec(memory_space=pl.ANY),
    )(place, *parts)
    key_value_gradient = key_value_gradient.reshape(
        1, slots, 2, length, KEY_VALUE_HEADS * HEAD_SIZE
    )
    return block_residual, query_gradient[None], key_value_gradient, weight_grad


def attention_backward(query_f, key_f, value_f, probs, rounded, grad_heads):
    prob_grad = jnp.einsum("mhqd,mhkd->mhqk", grad_heads, value_f, precision=lax.Precision.HIGHEST)
    delta = jnp.sum(prob_grad * probs, axis=-1, keepdims=True)
    score_grad = probs * (prob_grad - delta)
    query_gradient = jnp.einsum(
        "mhqk,mhkd->mhqd", score_grad, key_f, precision=lax.Precision.HIGHEST
    ) / math.sqrt(HEAD_SIZE)
    key_term = jnp.einsum(
        "mhqk,mhqd->mhkd", score_grad, query_f, precision=lax.Precision.HIGHEST
    ) / math.sqrt(HEAD_SIZE)
    value_term = jnp.einsum("mhqk,mhqd->mhkd", rounded, grad_heads, precision=lax.Precision.HIGHEST)
    return (query_gradient, key_term, value_term)


def by_weights(
    queries,
    slot_keys_values,
    segment_ids,
    residual_in,
    cotangent,
    out_weight,
    live_mask,
    micro_counts,
):
    tensor_size = lax.axis_size("tensor")
    heads_here = QUERY_HEADS // tensor_size
    heads_per_group = QUERY_HEADS // KEY_VALUE_HEADS
    tensor_idx = lax.axis_index("tensor")
    replica_idx = lax.axis_index("dp")
    query_here = queries[0]
    slot_total_count = query_here.shape[0]
    sequence_length = query_here.shape[1]
    local_feats = residual_in.shape[3]
    key_value_local = slot_keys_values[0].reshape(
        slot_total_count, 2, sequence_length, KEY_VALUE_HEADS, HEAD_SIZE
    )
    segments = segment_ids[0]
    head_ids = tensor_idx * heads_here + jnp.arange(heads_here)
    key_value_head_rows = head_ids // heads_per_group
    query_heads = query_here.reshape(
        slot_total_count, sequence_length, heads_here, HEAD_SIZE
    ).transpose(0, 2, 1, 3)
    key_head_rows = jnp.take(key_value_local[:, 0], key_value_head_rows, axis=2).transpose(
        0, 2, 1, 3
    )
    value_heads = jnp.take(key_value_local[:, 1], key_value_head_rows, axis=2).transpose(0, 2, 1, 3)
    positions = jnp.arange(sequence_length)
    allowed = (positions[None, :] <= positions[:, None])[None] & (
        segments[:, :, None] == segments[:, None, :]
    )
    allowed = allowed[:, None]
    scores = jnp.einsum(
        "mhqd,mhkd->mhqk", query_heads, key_head_rows, preferred_element_type=jnp.float32
    ) / math.sqrt(HEAD_SIZE)
    masked = jnp.where(allowed, scores, -jnp.inf)
    top_score = jnp.max(masked, axis=-1, keepdims=True)
    expo = jnp.where(allowed, jnp.exp(masked - top_score), 0.0)
    probs = expo / jnp.sum(expo, axis=-1, keepdims=True)
    probs_low = probs.astype(jnp.bfloat16)
    context = jnp.einsum(
        "mhqk,mhkd->mqhd", probs_low, value_heads, preferred_element_type=jnp.float32
    )
    context = context.astype(jnp.bfloat16).reshape(
        slot_total_count, sequence_length, heads_here * HEAD_SIZE
    )
    context_rows = context.reshape(slot_total_count * sequence_length, heads_here * HEAD_SIZE)
    weight_rows = lax.all_gather(out_weight, "dp", axis=1, tiled=True)
    reduced_total = lax.psum_scatter(
        jnp.einsum(
            "hd,nh->dn", weight_rows, context_rows, preferred_element_type=jnp.float32
        ).astype(jnp.bfloat16),
        "tensor",
        scatter_dimension=0,
        tiled=True,
    ).astype(jnp.float32)
    reduced_total = reduced_total.transpose(1, 0).reshape(
        slot_total_count, sequence_length, local_feats
    )
    block_residual = (residual_in[0].astype(jnp.float32) + reduced_total).astype(jnp.bfloat16)[None]
    replica_pick = jnp.arange(live_mask.shape[0]) == replica_idx
    my_live = jnp.sum(jnp.where(replica_pick, live_mask, 0))
    my_count = jnp.sum(jnp.where(replica_pick, micro_counts, 0))
    live_total = jnp.maximum(jnp.sum(live_mask * micro_counts), 1)
    slot_live = (jnp.arange(slot_total_count) < my_count) & (my_live > 0)
    slot_weight = slot_live.astype(jnp.float32) / live_total.astype(jnp.float32)
    scaled_cot = (cotangent[0].astype(jnp.float32) * slot_weight[:, None, None]).astype(
        jnp.bfloat16
    )
    weight_back = lax.all_gather(out_weight, "dp", axis=1, tiled=True)
    shard_piece = lax.all_gather(scaled_cot, "tensor", axis=2, tiled=True)
    grad_piece = jnp.einsum("msh,msd->hd", context, shard_piece, preferred_element_type=jnp.float32)
    grad_rows = grad_piece
    context_grad = jnp.einsum(
        "msd,hd->msh", shard_piece, weight_back, preferred_element_type=jnp.float32
    )
    grad_rows, context_grad = (grad_rows, context_grad)
    projection_weight_gradient = lax.psum_scatter(
        grad_rows.astype(jnp.bfloat16), "dp", scatter_dimension=1, tiled=True
    ).astype(jnp.float32)
    grad_heads = context_grad.reshape(
        slot_total_count, sequence_length, heads_here, HEAD_SIZE
    ).transpose(0, 2, 1, 3)
    query_f = query_heads.astype(jnp.float32)
    key_f = key_head_rows.astype(jnp.float32)
    value_f = value_heads.astype(jnp.float32)
    rounded = probs_low.astype(jnp.float32)
    query_gradient, key_term, value_term = attention_backward(
        query_f, key_f, value_f, probs, rounded, grad_heads
    )
    query_out = (
        query_gradient.transpose(0, 2, 1, 3)
        .reshape(slot_total_count, sequence_length, heads_here * HEAD_SIZE)
        .astype(jnp.bfloat16)[None]
    )
    addend_terms = (
        jnp.stack([key_term, value_term], axis=1).astype(jnp.bfloat16).astype(jnp.float32)
    )
    head_choice = (key_value_head_rows[:, None] == jnp.arange(KEY_VALUE_HEADS)[None, :]).astype(
        jnp.float32
    )
    positioned = jnp.einsum(
        "mchsd,hk->mcskd", addend_terms, head_choice, precision=lax.Precision.HIGHEST
    )
    positioned = positioned.reshape(
        slot_total_count, 2, sequence_length, KEY_VALUE_HEADS * HEAD_SIZE
    )
    keyval_sum = lax.psum(positioned.astype(jnp.bfloat16), "tensor")
    key_value_gradient = keyval_sum[None]
    return (block_residual, query_out, key_value_gradient, projection_weight_gradient)


def solution(mesh):
    dp_size, tensor_size = mesh.shape["dp"], mesh.shape["tensor"]
    regular = dp_size == 4 and tensor_size % 4 == 0 and tensor_size & (tensor_size - 1) == 0
    regular = regular and tensor_size == KEY_VALUE_HEADS
    per_device = functools.partial(by_activations, tensor_size) if regular else by_weights
    placed = (
        P("dp", None, None, "tensor"),
        P("dp", None, None, None, None),
        P("dp", None, None),
        P("dp", None, None, "tensor"),
        P("dp", None, None, "tensor"),
        P("tensor", "dp"),
        P(),
        P(),
    )
    return jax.shard_map(
        per_device,
        mesh=mesh,
        in_specs=placed,
        out_specs=(
            P("dp", None, None, "tensor"),
            P("dp", None, None, "tensor"),
            P("dp", None, None, None, None),
            P("tensor", "dp"),
        ),
        check_vma=False,
    )
```

```python
import functools
import math

import jax
import jax.numpy as jnp
from jax import lax
from jax.experimental import pallas as pl
from jax.experimental.pallas import tpu as pltpu
from jax.sharding import PartitionSpec as P

HEAD_SIZE = 128
QUERY_HEADS = 64
KEY_VALUE_HEADS = 8
BF = jnp.bfloat16
F32 = jnp.float32
VMEM = pl.BlockSpec(memory_space=pltpu.VMEM)
SMEM = pl.BlockSpec(memory_space=pltpu.SMEM)
NT = (((1,), (1,)), ((), ()))
TN = (((0,), (0,)), ((), ()))
NN = (((1,), (0,)), ((), ()))
LIMIT = 28 * 1024 * 1024


def dot(a, b, dims=NN):
    return lax.dot_general(a, b, dims, preferred_element_type=F32)


def call(kernel, out_shape, in_specs, flops, moved, scratch=(), **grid):
    return pl.pallas_call(
        kernel,
        out_shape=out_shape,
        in_specs=in_specs,
        scratch_shapes=scratch,
        cost_estimate=pl.CostEstimate(flops=flops, bytes_accessed=moved, transcendentals=0),
        compiler_params=pltpu.CompilerParams(vmem_limit_bytes=LIMIT),
        **grid,
    )


def stack_heads(rows, heads):
    return jnp.concatenate(
        [rows[:, h * HEAD_SIZE : (h + 1) * HEAD_SIZE] for h in range(heads)], axis=0
    )


def forward_kernel(heads, q_ref, key_value_ref, seg_ref, context_ref, probs_ref):
    slots, length = q_ref.shape[:2]
    row = lax.broadcasted_iota(jnp.int32, (length, length), 0)
    col = lax.broadcasted_iota(jnp.int32, (length, length), 1)
    for m in range(slots):
        seg = jnp.broadcast_to(seg_ref[m : m + 1, :].astype(F32), (length, length))
        allowed = (col <= row) & (seg == seg.T)
        q = stack_heads(q_ref[m], heads)
        scores = dot(q, key_value_ref[m, 0], NT) * (1.0 / math.sqrt(HEAD_SIZE))
        scores = scores.reshape(heads, length, length)
        masked = jnp.where(allowed[None], scores, -jnp.inf)
        expo = jnp.exp(masked - jnp.max(masked, axis=-1, keepdims=True))
        probs = expo / jnp.sum(expo, axis=-1, keepdims=True)
        probs = probs.reshape(heads * length, length)
        probs_ref[m] = probs
        context = dot(probs.astype(BF), key_value_ref[m, 1]).astype(BF)
        for h in range(heads):
            context_ref[m * length : (m + 1) * length, h * HEAD_SIZE : (h + 1) * HEAD_SIZE] = (
                context[h * length : (h + 1) * length]
            )


def backward_kernel(
    heads, own_ref, got_ref, q_ref, key_value_ref, probs_ref, query_grad_ref, key_value_grad_ref
):
    slots, length = q_ref.shape[:2]
    scale = 1.0 / math.sqrt(HEAD_SIZE)
    for m in range(slots):
        rows = slice(m * length, (m + 1) * length)
        grad = (own_ref[rows, :] + got_ref[rows, :].astype(F32)).astype(BF)
        grad = stack_heads(grad, heads)
        q = stack_heads(q_ref[m], heads)
        key, value = key_value_ref[m, 0], key_value_ref[m, 1]
        probs = probs_ref[m]
        prob_grad = dot(grad, value, NT)
        delta = jnp.sum(prob_grad * probs, axis=-1, keepdims=True)
        score_grad = probs * (prob_grad - delta)
        high = score_grad.astype(BF)
        low = (score_grad - high.astype(F32)).astype(BF)
        query_grad = ((dot(high, key) + dot(low, key)) * scale).astype(BF)
        for h in range(heads):
            query_grad_ref[m, :, h * HEAD_SIZE : (h + 1) * HEAD_SIZE] = query_grad[
                h * length : (h + 1) * length
            ]
        key_grad = (dot(high, q, TN) + dot(low, q, TN)) * scale
        key_value_grad_ref[m, 0] = key_grad.astype(BF)
        key_value_grad_ref[m, 1] = dot(probs.astype(BF), grad, TN).astype(BF)


def turn_kernel(cot_ref, out_ref, padded):
    slots, length, features = cot_ref.shape
    padded[:, features:] = jnp.zeros((slots * length, padded.shape[1] - features), F32)
    for m in range(slots):
        padded[m * length : (m + 1) * length, :features] = cot_ref[m].astype(F32)
    out_ref[...] = padded[...].T[:features].astype(BF)


def finish_kernel(kept_ref, got_ref, residual_ref, out_ref, padded):
    slots, length, features = residual_ref.shape
    padded[:features, :] = kept_ref[...].astype(F32) + got_ref[...].astype(F32)
    padded[features:, :] = jnp.zeros((padded.shape[0] - features, padded.shape[1]), F32)
    rows = padded[...].T
    for m in range(slots):
        out_ref[m] = (
            residual_ref[m].astype(F32) + rows[m * length : (m + 1) * length, :features]
        ).astype(BF)


def local_block(place_ref, mask, inner):
    core = place_ref[0] % 2
    index = (place_ref[1] % inner) ^ mask
    return ((index // (inner // 2)) ^ core) * (inner // 2) + index % (inner // 2)


def project_kernel(inner, place_ref, own_w, other_w, context_own, context_other, *refs):
    outs, total, turned = refs[:-2], refs[-2], refs[-1]
    step = pl.program_id(0)
    tokens = context_own.shape[0]
    features = own_w.shape[0]

    @pl.when(step == 0)
    def _():
        turned[:, :tokens] = context_own[...].T
        turned[:, tokens:] = context_other[...].T

    def rows(weight):
        at = pl.ds(pl.multiple_of(step * features, 16), features)
        total[at, :] = dot(weight, turned[...]).astype(BF)

    @pl.when(step < inner // 2)
    def _():
        rows(own_w[...])

    @pl.when(step >= inner // 2)
    def _():
        rows(other_w[...])

    @pl.when(step == inner - 1)
    def _():
        for mask in range(inner):
            at = pl.multiple_of(local_block(place_ref, mask, inner) * features, 16)
            block = total[pl.ds(at, features), :]
            outs[2 * mask][...] = block[:, :tokens]
            outs[2 * mask + 1][...] = block[:, tokens:]


def load_shards(inner, place_ref, shards, cot, first, sems):
    features, tokens = shards[0].shape
    copies = []
    for mask, shard in enumerate(shards):
        at = pl.multiple_of(local_block(place_ref, mask, inner) * features, 16)
        to = cot.at[pl.ds(at, features), pl.ds(first, tokens)]
        copies.append(pltpu.make_async_copy(shard, to, sems.at[first // tokens, mask]))
        copies[-1].start()
    return copies


def context_grad_kernel(inner, place_ref, own_w, other_w, *refs):
    shards, (out_ref, cot, turned, sems) = refs[:inner], refs[-4:]
    own_rows = own_w.shape[0]

    @pl.when(pl.program_id(0) == 0)
    def _():
        for copy in load_shards(inner, place_ref, shards, cot, 0, sems):
            copy.wait()
        turned[0] = cot[:own_rows, :].T
        turned[1] = cot[own_rows:, :].T

    total = dot(turned[0], own_w[...]) + dot(turned[1], other_w[...])
    out_ref[...] = total.astype(out_ref.dtype)


def weight_grad_kernel(inner, place_ref, context_own, context_other, *refs):
    shards, (own_ref, other_ref, cot, sems) = refs[: 2 * inner], refs[-4:]
    own_rows = own_ref.shape[0]
    tokens = context_own.shape[0]

    @pl.when(pl.program_id(0) == 0)
    def _():
        copies = load_shards(inner, place_ref, shards[:inner], cot, 0, sems)
        copies += load_shards(inner, place_ref, shards[inner:], cot, tokens, sems)
        for copy in copies:
            copy.wait()

    def rows(start):
        return dot(cot[start : start + own_rows, :tokens], context_own[...]) + dot(
            cot[start : start + own_rows, tokens:], context_other[...]
        )

    own_ref[...] = rows(0)
    other_ref[...] = rows(own_rows).astype(BF)


def place_kernel(place_ref, *refs):
    shards, (out_ref, sems) = refs[:-2], refs[-2:]
    copies = []
    for mask, shard in enumerate(shards):
        at = pl.multiple_of((place_ref[1] ^ mask) * HEAD_SIZE, HEAD_SIZE)
        copies.append(
            pltpu.make_async_copy(shard, out_ref.at[:, pl.ds(at, HEAD_SIZE)], sems.at[mask])
        )
    for copy in copies:
        copy.start()
    for copy in copies:
        copy.wait()


def slot_weights(live_mask, micro_counts, slots):
    replica = lax.axis_index("dp")
    pick = jnp.arange(live_mask.shape[0]) == replica
    my_live = jnp.sum(jnp.where(pick, live_mask, 0))
    my_count = jnp.sum(jnp.where(pick, micro_counts, 0))
    live_total = jnp.maximum(jnp.sum(live_mask * micro_counts), 1)
    slot_live = (jnp.arange(slots) < my_count) & (my_live > 0)
    return slot_live.astype(F32) / live_total.astype(F32)


def by_activations(
    tensor_size,
    queries,
    slot_keys_values,
    segment_ids,
    residual_in,
    cotangent,
    out_weight,
    live_mask,
    micro_counts,
):
    inner = tensor_size // 2
    _, slots, length, width = queries.shape
    features = residual_in.shape[3]
    heads = width // HEAD_SIZE
    tokens = slots * length
    dp_idx, tensor_idx = lax.axis_index("dp"), lax.axis_index("tensor")
    place = jnp.stack([dp_idx, tensor_idx]).astype(jnp.int32)
    home = (dp_idx // 2) == (tensor_idx // inner)

    def swap(array, mask):
        return lax.ppermute(array, "tensor", [(t, t ^ mask) for t in range(tensor_size)])

    def swap_x(array):
        return lax.ppermute(array, "dp", [(d, d ^ 2) for d in range(4)])

    def swap_core(array):
        return lax.ppermute(array, "dp", [(d, d ^ 1) for d in range(4)])

    shape = jax.ShapeDtypeStruct
    wide = (features + 127) // 128 * 128

    turned = call(
        turn_kernel,
        shape((features, tokens), BF),
        [pl.BlockSpec(cotangent.shape[1:])],
        0,
        4 * tokens * features,
        [pltpu.VMEM((tokens, wide), F32)],
    )(cotangent[0])
    across = swap(turned, inner)

    weight_own = out_weight.T
    weight_other = swap_core(weight_own)
    own_rows = weight_own.shape[0]

    key_value = lax.dynamic_slice_in_dim(
        slot_keys_values[0], tensor_idx * HEAD_SIZE, HEAD_SIZE, axis=3
    )
    context, probs = call(
        functools.partial(forward_kernel, heads),
        (
            shape((tokens, width), BF),
            shape((slots, heads * length, length), F32),
        ),
        [pl.BlockSpec((slots, length, width)), pl.BlockSpec((slots, 2, length, HEAD_SIZE)), pl.BlockSpec((slots, length))],
        4 * tokens * width * length,
        4 * tokens * width * 2,
    )(queries[0], key_value, segment_ids[0])
    context_other = swap_x(context)
    across, context = lax.optimization_barrier((across, context))
    weight = jnp.repeat(slot_weights(live_mask, micro_counts, slots), length)
    scaled = lambda array: (array.astype(F32) * weight[None, :]).astype(BF)
    sent = scaled(jnp.where(home, across, turned))
    cot_other = swap_x(sent)
    across, _ = lax.optimization_barrier((across, sent))
    cot_own = scaled(jnp.where(home, turned, across))
    shards_own = [swap(cot_own, mask) if mask else cot_own for mask in range(inner)]


    cot_other, context_other = lax.optimization_barrier((cot_other, context_other))

    big = 2 * tokens * width * 2 * own_rows
    whole = lambda *dims: pl.BlockSpec(dims, lambda i: (0,) * len(dims))
    anywhere = pl.BlockSpec(memory_space=pl.ANY)
    half = inner // 2
    partial = call(
        functools.partial(project_kernel, inner),
        [shape((features, tokens), BF)] * (2 * inner),
        [
            SMEM,
            pl.BlockSpec((features, width), lambda i: (jnp.minimum(i, half - 1), 0)),
            pl.BlockSpec((features, width), lambda i: (jnp.maximum(i - half, 0), 0)),
            whole(tokens, width),
            whole(tokens, width),
        ],
        2 * big,
        4 * own_rows * width,
        [pltpu.VMEM((2 * own_rows, 2 * tokens), BF), pltpu.VMEM((width, 2 * tokens), BF)],
        out_specs=[whole(features, tokens)] * (2 * inner),
        grid=(inner,),
    )(place, weight_own, weight_other, context, context_other)
    shards_other = [swap(cot_other, mask) if mask else cot_other for mask in range(inner)]
    near, far = list(partial[::2]), partial[1::2]
    far = [swap(far[mask], mask) if mask else far[mask] for mask in range(inner)]

    tile = min(1024, width)
    column = lambda rows: pl.BlockSpec((rows, tile), lambda i: (0, i))

    def context_grad(shards, dtype):
        return call(
            functools.partial(context_grad_kernel, inner),
            shape((tokens, width), dtype),
            [SMEM, column(own_rows), column(own_rows)] + [anywhere] * len(shards),
            big,
            4 * own_rows * width,
            [
                pltpu.VMEM((2 * own_rows, tokens), BF),
                pltpu.VMEM((2, tokens, own_rows), BF),
                pltpu.SemaphoreType.DMA((1, inner)),
            ],
            out_specs=column(tokens),
            grid=(width // tile,),
        )(place, weight_own, weight_other, *shards)

    grad_own = context_grad(shards_own, F32)
    grad_other = context_grad(shards_other + [grad_own], BF)
    grad_got = swap_x(grad_other)

    *near, _ = lax.optimization_barrier((*near, grad_other))
    near = [swap(near[mask], mask) if mask else near[mask] for mask in range(inner)]
    add = lambda blocks: sum(block.astype(F32) for block in blocks).astype(BF)
    near_sum, far_sum = add(near), add(far)
    far_got = swap_x(far_sum)

    far_sum, context_late = lax.optimization_barrier((far_sum, context))
    weight_grad, weight_grad_other = call(
        functools.partial(weight_grad_kernel, inner),
        (
            shape((own_rows, width), F32),
            shape((own_rows, width), BF),
        ),
        [SMEM, column(tokens), column(tokens)] + [anywhere] * (2 * inner + 1),
        2 * big,
        6 * own_rows * width,
        [
            pltpu.VMEM((2 * own_rows, 2 * tokens), BF),
            pltpu.SemaphoreType.DMA((2, inner)),
        ],
        out_specs=(column(own_rows), column(own_rows)),
        grid=(width // tile,),
    )(place, context_late, context_other, *shards_own, *shards_other, grad_other)
    grad_got, weight_grad_other, near_sum, far_got = lax.optimization_barrier(
        (grad_got, weight_grad_other, near_sum, far_got)
    )
    query_gradient, key_value_part = call(
        functools.partial(backward_kernel, heads),
        (
            shape((slots, length, width), BF),
            shape((slots, 2, length, HEAD_SIZE), BF),
        ),
        [VMEM] * 5,
        14 * tokens * width * length,
        8 * tokens * width * 2,
    )(grad_own, grad_got, queries[0], key_value, probs)
    weight_grad = (weight_grad + swap_core(weight_grad_other).astype(F32)).T

    rows = slots * 2 * length
    part = key_value_part.reshape(rows, HEAD_SIZE)
    parts = [swap(part, mask) if mask else part for mask in range(inner)]
    part = swap(part, inner)
    part, weight_grad = lax.optimization_barrier((part, weight_grad))
    parts += [swap(part, mask) if mask else part for mask in range(inner)]
    kept = jnp.where(home, near_sum, far_got)
    got = swap(jnp.where(home, far_got, near_sum), inner)
    got, parts[1], parts[2], parts[3] = lax.optimization_barrier((got, parts[1], parts[2], parts[3]))
    block_residual = call(
        finish_kernel,
        shape((slots, length, features), BF),
        [VMEM] * 3,
        0,
        8 * tokens * features,
        [pltpu.VMEM((wide, tokens), F32)],
    )(kept, got, residual_in[0])[None]
    key_value_gradient = call(
        place_kernel,
        shape((rows, KEY_VALUE_HEADS * HEAD_SIZE), BF),
        [SMEM] + [pl.BlockSpec(memory_space=pl.ANY)] * tensor_size,
        0,
        2 * rows * KEY_VALUE_HEADS * HEAD_SIZE,
        [pltpu.SemaphoreType.DMA((tensor_size,))],
        out_specs=pl.BlockSpec(memory_space=pl.ANY),
    )(place, *parts)
    key_value_gradient = key_value_gradient.reshape(
        1, slots, 2, length, KEY_VALUE_HEADS * HEAD_SIZE
    )
    return block_residual, query_gradient[None], key_value_gradient, weight_grad


def attention_backward(query_f, key_f, value_f, probs, rounded, grad_heads):
    prob_grad = jnp.einsum("mhqd,mhkd->mhqk", grad_heads, value_f, precision=lax.Precision.HIGHEST)
    delta = jnp.sum(prob_grad * probs, axis=-1, keepdims=True)
    score_grad = probs * (prob_grad - delta)
    query_gradient = jnp.einsum(
        "mhqk,mhkd->mhqd", score_grad, key_f, precision=lax.Precision.HIGHEST
    ) / math.sqrt(HEAD_SIZE)
    key_term = jnp.einsum(
        "mhqk,mhqd->mhkd", score_grad, query_f, precision=lax.Precision.HIGHEST
    ) / math.sqrt(HEAD_SIZE)
    value_term = jnp.einsum("mhqk,mhqd->mhkd", rounded, grad_heads, precision=lax.Precision.HIGHEST)
    return (query_gradient, key_term, value_term)


def by_weights(
    queries,
    slot_keys_values,
    segment_ids,
    residual_in,
    cotangent,
    out_weight,
    live_mask,
    micro_counts,
):
    tensor_size = lax.axis_size("tensor")
    heads_here = QUERY_HEADS // tensor_size
    heads_per_group = QUERY_HEADS // KEY_VALUE_HEADS
    tensor_idx = lax.axis_index("tensor")
    replica_idx = lax.axis_index("dp")
    query_here = queries[0]
    slot_total_count = query_here.shape[0]
    sequence_length = query_here.shape[1]
    local_feats = residual_in.shape[3]
    key_value_local = slot_keys_values[0].reshape(
        slot_total_count, 2, sequence_length, KEY_VALUE_HEADS, HEAD_SIZE
    )
    segments = segment_ids[0]
    head_ids = tensor_idx * heads_here + jnp.arange(heads_here)
    key_value_head_rows = head_ids // heads_per_group
    query_heads = query_here.reshape(
        slot_total_count, sequence_length, heads_here, HEAD_SIZE
    ).transpose(0, 2, 1, 3)
    key_head_rows = jnp.take(key_value_local[:, 0], key_value_head_rows, axis=2).transpose(
        0, 2, 1, 3
    )
    value_heads = jnp.take(key_value_local[:, 1], key_value_head_rows, axis=2).transpose(0, 2, 1, 3)
    positions = jnp.arange(sequence_length)
    allowed = (positions[None, :] <= positions[:, None])[None] & (
        segments[:, :, None] == segments[:, None, :]
    )
    allowed = allowed[:, None]
    scores = jnp.einsum(
        "mhqd,mhkd->mhqk", query_heads, key_head_rows, preferred_element_type=jnp.float32
    ) / math.sqrt(HEAD_SIZE)
    masked = jnp.where(allowed, scores, -jnp.inf)
    top_score = jnp.max(masked, axis=-1, keepdims=True)
    expo = jnp.where(allowed, jnp.exp(masked - top_score), 0.0)
    probs = expo / jnp.sum(expo, axis=-1, keepdims=True)
    probs_low = probs.astype(jnp.bfloat16)
    context = jnp.einsum(
        "mhqk,mhkd->mqhd", probs_low, value_heads, preferred_element_type=jnp.float32
    )
    context = context.astype(jnp.bfloat16).reshape(
        slot_total_count, sequence_length, heads_here * HEAD_SIZE
    )
    context_rows = context.reshape(slot_total_count * sequence_length, heads_here * HEAD_SIZE)
    weight_rows = lax.all_gather(out_weight, "dp", axis=1, tiled=True)
    reduced_total = lax.psum_scatter(
        jnp.einsum(
            "hd,nh->dn", weight_rows, context_rows, preferred_element_type=jnp.float32
        ).astype(jnp.bfloat16),
        "tensor",
        scatter_dimension=0,
        tiled=True,
    ).astype(jnp.float32)
    reduced_total = reduced_total.transpose(1, 0).reshape(
        slot_total_count, sequence_length, local_feats
    )
    block_residual = (residual_in[0].astype(jnp.float32) + reduced_total).astype(jnp.bfloat16)[None]
    replica_pick = jnp.arange(live_mask.shape[0]) == replica_idx
    my_live = jnp.sum(jnp.where(replica_pick, live_mask, 0))
    my_count = jnp.sum(jnp.where(replica_pick, micro_counts, 0))
    live_total = jnp.maximum(jnp.sum(live_mask * micro_counts), 1)
    slot_live = (jnp.arange(slot_total_count) < my_count) & (my_live > 0)
    slot_weight = slot_live.astype(jnp.float32) / live_total.astype(jnp.float32)
    scaled_cot = (cotangent[0].astype(jnp.float32) * slot_weight[:, None, None]).astype(
        jnp.bfloat16
    )
    weight_back = lax.all_gather(out_weight, "dp", axis=1, tiled=True)
    shard_piece = lax.all_gather(scaled_cot, "tensor", axis=2, tiled=True)
    grad_piece = jnp.einsum("msh,msd->hd", context, shard_piece, preferred_element_type=jnp.float32)
    grad_rows = grad_piece
    context_grad = jnp.einsum(
        "msd,hd->msh", shard_piece, weight_back, preferred_element_type=jnp.float32
    )
    grad_rows, context_grad = (grad_rows, context_grad)
    projection_weight_gradient = lax.psum_scatter(
        grad_rows.astype(jnp.bfloat16), "dp", scatter_dimension=1, tiled=True
    ).astype(jnp.float32)
    grad_heads = context_grad.reshape(
        slot_total_count, sequence_length, heads_here, HEAD_SIZE
    ).transpose(0, 2, 1, 3)
    query_f = query_heads.astype(jnp.float32)
    key_f = key_head_rows.astype(jnp.float32)
    value_f = value_heads.astype(jnp.float32)
    rounded = probs_low.astype(jnp.float32)
    query_gradient, key_term, value_term = attention_backward(
        query_f, key_f, value_f, probs, rounded, grad_heads
    )
    query_out = (
        query_gradient.transpose(0, 2, 1, 3)
        .reshape(slot_total_count, sequence_length, heads_here * HEAD_SIZE)
        .astype(jnp.bfloat16)[None]
    )
    addend_terms = (
        jnp.stack([key_term, value_term], axis=1).astype(jnp.bfloat16).astype(jnp.float32)
    )
    head_choice = (key_value_head_rows[:, None] == jnp.arange(KEY_VALUE_HEADS)[None, :]).astype(
        jnp.float32
    )
    positioned = jnp.einsum(
        "mchsd,hk->mcskd", addend_terms, head_choice, precision=lax.Precision.HIGHEST
    )
    positioned = positioned.reshape(
        slot_total_count, 2, sequence_length, KEY_VALUE_HEADS * HEAD_SIZE
    )
    keyval_sum = lax.psum(positioned.astype(jnp.bfloat16), "tensor")
    key_value_gradient = keyval_sum[None]
    return (block_residual, query_out, key_value_gradient, projection_weight_gradient)


def solution(mesh):
    dp_size, tensor_size = mesh.shape["dp"], mesh.shape["tensor"]
    regular = dp_size == 4 and tensor_size % 4 == 0 and tensor_size & (tensor_size - 1) == 0
    regular = regular and tensor_size == KEY_VALUE_HEADS
    per_device = functools.partial(by_activations, tensor_size) if regular else by_weights
    placed = (
        P("dp", None, None, "tensor"),
        P("dp", None, None, None, None),
        P("dp", None, None),
        P("dp", None, None, "tensor"),
        P("dp", None, None, "tensor"),
        P("tensor", "dp"),
        P(),
        P(),
    )
    return jax.shard_map(
        per_device,
        mesh=mesh,
        in_specs=placed,
        out_specs=(
            P("dp", None, None, "tensor"),
            P("dp", None, None, "tensor"),
            P("dp", None, None, None, None),
            P("tensor", "dp"),
        ),
        check_vma=False,
    )
```
